32 devices in a mesh: section: 2 (over x), ctx: 4 (over z), fsdp: 4 (over y, core).
Axes of the slice: x: 2, y: 2, z: 4, core: 2. Of those that a mesh axis runs over, the one named last changes fastest.
Arguments:
- inputs: bfloat16 [4, 512, 2, 1536], P(None, ('ctx', 'fsdp')), may hold values from -6 to 6
- cotangent: bfloat16 [4, 512, 2, 1536], P(None, ('ctx', 'fsdp')), may hold values from -6 to 6
- attn_gain: bfloat16 [2, 1536], P('section', 'fsdp'), may hold values from 0.099609375 to 1.8984375
- qkv_weight: bfloat16 [2, 1536, 2048], P('section', 'fsdp'), may hold values from -0.15625 to 0.15625
- qkv_bias: bfloat16 [2, 2048], P('section', 'fsdp'), may hold values from -1.75 to 1.75
- out_weight: bfloat16 [2, 1536, 1536], P('section', 'fsdp'), may hold values from -0.5 to 0.5
- mlp_gain: bfloat16 [2, 1536], P('section', 'fsdp'), may hold values from 0.099609375 to 1.8984375
- gate_weight: bfloat16 [2, 8960, 1536], P('section', 'fsdp'), may hold values from -0.15625 to 0.15625
- up_weight: bfloat16 [2, 8960, 1536], P('section', 'fsdp'), may hold values from -0.15625 to 0.15625
- down_weight: bfloat16 [2, 8960, 1536], P('section', 'fsdp'), may hold values from -0.0625 to 0.0625
Outputs:
- layer_outputs: bfloat16 [2, 4, 512, 2, 1536], P('section', None, ('ctx', 'fsdp'))
- input_grads: bfloat16 [2, 4, 512, 2, 1536], P('section', None, ('ctx', 'fsdp'))
- attn_gain_grad: float32 [2, 1536], P('section', 'fsdp')
- qkv_weight_grad: float32 [2, 1536, 2048], P('section', 'fsdp')
- qkv_bias_grad: float32 [2, 1792], P('section', 'fsdp')
- value_bias_grad: float32 [2, 256], P('section', 'fsdp')
- out_weight_grad: float32 [2, 1536, 1536], P('section', 'fsdp')
- mlp_gain_grad: float32 [2, 1536], P('section', 'fsdp')
- gate_weight_grad: float32 [2, 8960, 1536], P('section', 'fsdp')
- up_weight_grad: float32 [2, 8960, 1536], P('section', 'fsdp')
- down_weight_grad: float32 [2, 8960, 1536], P('section', 'fsdp')
The draws below stay inside these ranges and needn't reach their ends.
All inputs are finite; a program needn't handle non-finite values.
Results may differ from the reference program's by a relative error of at most 0.028.
Values may be sent and summed in bfloat16 or wider, within the bound.
No kernel may reach another device: no remote copies, remote signals or barrier semaphores. Data moves between devices by JAX's collectives and lax.ppermute only.
A program may use at most 512 MiB of HBM per device.

```python
import math
import jax
import jax.numpy as jnp
from jax import lax

D = 1536
HEADS = 12
KV_HEADS = 2
HEAD_DIM = 128
FF = 8960
LAYERS = 2
MICRO = 4
QKV = 2048
SPAN = 128
HALF = 512
LENGTH = 1024


def block_scale(key, extent, split, smallest, top_value):
    gain = 1.0
    for axis_at, blocks in split:
        steps = jax.random.uniform(jax.random.fold_in(jax.random.fold_in(key, 6), axis_at), (blocks,), jnp.float32, smallest / len(split), top_value / len(split))
        gain = gain * jnp.repeat(jnp.exp(steps), extent[axis_at] // blocks).reshape((-1,) + (1,) * (len(extent) - 1 - axis_at))
    return gain


def noise(own_key, shape, scale, bound, split=(), kind=jnp.bfloat16):
    level = block_scale(own_key, shape, split, -0.22, 0.18) if split else 1.0
    entries = jax.random.normal(own_key, shape, jnp.float32) * scale * level
    return jnp.minimum(jnp.maximum(entries, -bound), bound).astype(kind)


def setup_inputs(seed: int = 0) -> dict:
    seeds = jax.random.split(jax.random.key(seed), 11)
    inputs = noise(seeds[0], (MICRO, HALF, 2, D), 1.0, 6.0, ((1, 16),))
    cotangent = noise(seeds[1], (MICRO, HALF, 2, D), 1.0, 6.0, ((1, 16),))
    attn_gain = jnp.clip(1.0 + 0.18 * jax.random.normal(seeds[2], (LAYERS, D), jnp.float32), 0.099609375, 1.8984375).astype(jnp.bfloat16)
    qkv_weight = noise(seeds[3], (LAYERS, D, QKV), D ** -0.5, 0.15625, ((0, 2), (1, 4)))
    qkv_bias = noise(seeds[4], (LAYERS, QKV), 0.3, 1.75, ((0, 2), (1, 4)))
    out_weight = noise(seeds[5], (LAYERS, HEADS * HEAD_DIM, D), HEAD_DIM ** -0.5, 0.5, ((0, 2), (1, 4)))
    mlp_gain = jnp.clip(1.0 + 0.18 * jax.random.normal(seeds[6], (LAYERS, D), jnp.float32), 0.099609375, 1.8984375).astype(jnp.bfloat16)
    gate_weight = noise(seeds[7], (LAYERS, FF, D), D ** -0.5, 0.15625, ((0, 2), (1, 4)))
    up_weight = noise(seeds[8], (LAYERS, FF, D), D ** -0.5, 0.15625, ((0, 2), (1, 4)))
    down_weight = noise(seeds[9], (LAYERS, FF, D), FF ** -0.5, 0.0625, ((0, 2), (1, 4)))
    return {"inputs": inputs, "cotangent": cotangent, "attn_gain": attn_gain, "qkv_weight": qkv_weight, "qkv_bias": qkv_bias, "out_weight": out_weight, "mlp_gain": mlp_gain, "gate_weight": gate_weight, "up_weight": up_weight, "down_weight": down_weight}


@jax.custom_vjp
def low(v):
    return lax.optimization_barrier(v.astype(jnp.bfloat16)).astype(jnp.float32)

@jax.custom_vjp
def low_back(v):
    return v

def low_keep(v):
    return (low(v), None)

def low_pass(kept, grad):
    return (grad,)

def back_keep(v):
    return (v, None)

def back_low(kept, grad):
    return (low(grad),)
low.defvjp(low_keep, low_pass)
low_back.defvjp(back_keep, back_low)
epsilon = 1e-06
rope_base = 1000000.0
negative = -1e+30
highest = lax.Precision.HIGHEST

def storage_place(indices, span_rows, half_rows):
    second = 2 * half_rows - span_rows * (indices // span_rows + 1) + indices % span_rows
    return jnp.stack([indices, second], axis=-1)

def rotate(values, places, direction):
    half_width = values.shape[-1] // 2
    frequency = rope_base ** (-(jnp.arange(half_width, dtype=jnp.float32) * 2.0) / (2 * half_width))
    angles = places.astype(jnp.float32)[..., None, None] * frequency
    cosine = jnp.cos(angles)
    sine_part = jnp.sin(angles) * direction
    leading = values[..., :half_width]
    trailing = values[..., half_width:]
    return jnp.concatenate([leading * cosine - trailing * sine_part, trailing * cosine + leading * sine_part], axis=-1)

def inverse_rms(values):
    return lax.rsqrt(lax.optimization_barrier(jnp.mean(values * values, axis=-1, keepdims=True)) + epsilon)

def product(former, latter):
    return jnp.dot(former, latter, precision=highest, preferred_element_type=jnp.float32)

def attention(queries, keys, values, places):
    block_rows = math.gcd(LENGTH, 512)
    group_size = HEADS // KV_HEADS
    query_blocks = queries.reshape(LENGTH // block_rows, block_rows, KV_HEADS, group_size, HEAD_DIM)
    place_blocks = places.reshape(LENGTH // block_rows, block_rows)

    def one_block(pieces):
        query_block, place_block = pieces
        scores = low_back(jnp.einsum('qgjd,kgd->gjqk', query_block, keys, precision=highest)) * HEAD_DIM ** (-0.5)
        allowed = places[None, :] <= place_block[:, None]
        scores = jnp.where(allowed[None, None], scores, negative)
        probs_block = low(jax.nn.softmax(scores, axis=-1))
        return jnp.einsum('gjqk,kgd->qgjd', probs_block, values, precision=highest)
    attended = lax.map(jax.checkpoint(one_block), (query_blocks, place_blocks))
    return attended.reshape(LENGTH, HEADS * HEAD_DIM)

def layer_forward(source, params, places):
    attn_gain, qkv_weight, qkv_bias, out_weight, mlp_gain, gate_weight, up_weight, down_weight = params
    normed = low(source * inverse_rms(source) * attn_gain)
    projected = low_back(product(normed, qkv_weight) + qkv_bias)
    query_cols = HEADS * HEAD_DIM
    kv_cols = KV_HEADS * HEAD_DIM
    queries = low(rotate(projected[:, :query_cols].reshape(LENGTH, HEADS, HEAD_DIM), places, 1.0))
    keys = low(rotate(projected[:, query_cols:query_cols + kv_cols].reshape(LENGTH, KV_HEADS, HEAD_DIM), places, 1.0))
    values = low(projected[:, query_cols + kv_cols:].reshape(LENGTH, KV_HEADS, HEAD_DIM))
    attended = low(low_back(attention(queries, keys, values, places)))
    hidden = source + low_back(product(attended, out_weight))
    normed_two = low(hidden * inverse_rms(hidden) * mlp_gain)
    gate_pre = low_back(product(normed_two, gate_weight.T))
    up_pre = low_back(product(normed_two, up_weight.T))
    activated = low(jax.nn.silu(gate_pre) * up_pre)
    return hidden + low_back(product(activated, down_weight))

def reference(inputs, cotangent, attn_gain, qkv_weight, qkv_bias, out_weight, mlp_gain, gate_weight, up_weight, down_weight):
    places = storage_place(jnp.arange(HALF, dtype=jnp.int32), SPAN, HALF).reshape(LENGTH)
    params = tuple((weight.astype(jnp.float32) for weight in (attn_gain, qkv_weight, qkv_bias, out_weight, mlp_gain, gate_weight, up_weight, down_weight)))
    first_params = tuple((weight[0] for weight in params))
    second_params = tuple((weight[1] for weight in params))
    sequences = inputs.astype(jnp.float32).reshape(MICRO, LENGTH, D)
    tangents = cotangent.astype(jnp.float32).reshape(MICRO, LENGTH, D)

    def lower_layer(source, weights):
        return low(low_back(layer_forward(source, weights, places)))

    def upper_layer(source, weights):
        return layer_forward(source, weights, places)

    def one_sequence(totals, pieces):
        sequence, tangent = pieces
        middle, lower_back = jax.vjp(lower_layer, sequence, first_params)
        top_output, upper_back = jax.vjp(upper_layer, middle, second_params)
        grad_middle, from_upper = upper_back(tangent)
        grad_first, from_lower = lower_back(grad_middle)
        totals = tuple((summed + jnp.stack([early, late]) for summed, early, late in zip(totals, from_lower, from_upper)))
        return (totals, (jnp.stack([middle, top_output]), jnp.stack([grad_first, grad_middle])))
    initial = tuple((jnp.zeros_like(weight) for weight in params))
    totals, (states, grad_pairs) = lax.scan(one_sequence, initial, (sequences, tangents))
    layer_outputs = jnp.swapaxes(states, 0, 1).reshape(LAYERS, MICRO, HALF, 2, D).astype(jnp.bfloat16)
    input_grads = jnp.swapaxes(grad_pairs, 0, 1).reshape(LAYERS, MICRO, HALF, 2, D).astype(jnp.bfloat16)
    leading_cols = (HEADS + KV_HEADS) * HEAD_DIM
    bias_total = totals[2]
    return (layer_outputs, input_grads, totals[0], totals[1], bias_total[:, :leading_cols], bias_total[:, leading_cols:], totals[3], totals[4], totals[5], totals[6], totals[7])
```

```python
import functools
import math

import jax
import jax.numpy as jnp
from jax import lax
from jax.experimental import pallas as pl
from jax.experimental.pallas import tpu as pltpu
from jax.sharding import PartitionSpec as P

HEADS = 12
KV_HEADS = 2
HEAD_DIM = 128
GROUP = HEADS // KV_HEADS
EPS = 1e-06
ROPE_BASE = 1000000.0
NEGATIVE = -1e30
QCOLS = HEADS * HEAD_DIM
KCOLS = KV_HEADS * HEAD_DIM
SCALE = HEAD_DIM ** (-0.5)

MICROS = 1
LAG = 2

f32 = jnp.float32
bf16 = jnp.bfloat16
MIB = 1 << 20


def dot_nn(a, b):
    return lax.dot_general(a, b, (((1,), (0,)), ((), ())), preferred_element_type=f32)


def dot_nt(a, b):
    return lax.dot_general(a, b, (((1,), (1,)), ((), ())), preferred_element_type=f32)


def dot_tn(a, b):
    return lax.dot_general(a, b, (((0,), (0,)), ((), ())), preferred_element_type=f32)


def inverse_rms(values):
    return lax.rsqrt(jnp.mean(values * values, axis=-1, keepdims=True) + EPS)


def norm_backward(grad_normed, values, gain):
    inverse = inverse_rms(values)
    scaled = grad_normed * gain
    grad_values = inverse * scaled - values * (
        inverse**3 * jnp.mean(scaled * values, axis=-1, keepdims=True)
    )
    grad_gain = jnp.sum(grad_normed * values * inverse, axis=0, keepdims=True)
    return grad_values, grad_gain


def storage_place(indices, span_rows, half_rows):
    second = 2 * half_rows - span_rows * (indices // span_rows + 1) + indices % span_rows
    return jnp.stack([indices, second], axis=-1)


def exchange(block, axis, mask):
    size = lax.axis_size(axis)
    return lax.ppermute(block, axis, [(i, i ^ mask) for i in range(size)])


def passed_along(block, axis, distance):
    devices = range(lax.axis_size(axis))
    route = [(i - distance, i) for i in devices if i - distance in devices]
    return lax.ppermute(block, axis, route)


def bits_of(size):
    return [1 << b for b in reversed(range(size.bit_length() - 1))]


def relative_order(size):
    order = [0]
    for bit in bits_of(size):
        order = order + [r ^ bit for r in order]
    return order


def gather_pieces(block, axis):
    pieces = [block]
    for bit in bits_of(lax.axis_size(axis)):
        pieces = pieces + [exchange(p, axis, bit) for p in pieces]
    return pieces


def add_low(terms):
    total = terms[0].astype(f32)
    for term in terms[1:]:
        total = total + term.astype(f32)
    return total.astype(bf16)


def reduce_pieces(parts, axis):
    terms = [[p] for p in parts]
    for bit in reversed(bits_of(lax.axis_size(axis))):
        half = len(terms) // 2
        sent = [t[0] if len(t) == 1 else add_low(t) for t in terms[half:]]
        terms = [t + [exchange(s, axis, bit)] for t, s in zip(terms[:half], sent)]
    return terms[0]


def call(kernel, out_shape, args, flops, moved, name, limit=40, **kwargs):
    return pl.pallas_call(
        kernel,
        out_shape=out_shape,
        compiler_params=pltpu.CompilerParams(vmem_limit_bytes=limit * MIB),
        cost_estimate=pl.CostEstimate(flops=flops, bytes_accessed=moved, transcendentals=0),
        name=name,
        **kwargs,
    )(*args)


def turn(value, cos, sin):
    return value * cos + pltpu.roll(value, HEAD_DIM // 2, 1) * sin


def repeat_rows(table, count):
    return table if count == 1 else jnp.concatenate([table] * count, axis=0)


def project_kernel(reps, x_ref, gain_ref, w_ref, b_ref, cos_ref, sin_ref, q_ref, kv_ref, n_ref):
    step = pl.program_id(0)

    @pl.when(step == 0)
    def _():
        x = x_ref[...].astype(f32)
        n_ref[...] = (x * inverse_rms(x) * gain_ref[...].astype(f32)).astype(bf16)

    cos = repeat_rows(cos_ref[...], reps)
    sin = repeat_rows(sin_ref[...], reps)
    heads_here = w_ref.shape[1] // HEAD_DIM
    projected = dot_nn(n_ref[...], w_ref[...]) + b_ref[...].astype(f32)
    turned = []
    for j in range(heads_here):
        part = projected[:, j * HEAD_DIM : (j + 1) * HEAD_DIM]
        is_value = step * heads_here + j >= HEADS + KV_HEADS
        turned.append(jnp.where(is_value, part, turn(part, cos, sin)))
    low = jnp.concatenate(turned, axis=1).astype(bf16)

    @pl.when(step < pl.num_programs(0) - 1)
    def _():
        q_ref[...] = low

    @pl.when(step == pl.num_programs(0) - 1)
    def _():
        kv_ref[...] = low


def project(x, gain, w, b, cos, sin, reps):
    tokens, width = x.shape
    columns = w.shape[1]
    tile = 2 * KCOLS
    steps = columns // tile
    last_q = QCOLS // tile - 1
    return call(
        functools.partial(project_kernel, reps),
        (
            jax.ShapeDtypeStruct((tokens, QCOLS), bf16),
            jax.ShapeDtypeStruct((tokens, 2 * KCOLS), bf16),
        ),
        (x, gain, w, b, cos, sin),
        2 * tokens * width * columns,
        2 * width * columns,
        "project",
        grid=(steps,),
        in_specs=[
            pl.BlockSpec((tokens, width), lambda i: (0, 0)),
            pl.BlockSpec((1, width), lambda i: (0, 0)),
            pl.BlockSpec((width, tile), lambda i: (0, i)),
            pl.BlockSpec((1, tile), lambda i: (0, i)),
            pl.BlockSpec(cos.shape, lambda i: (0, 0)),
            pl.BlockSpec(sin.shape, lambda i: (0, 0)),
        ],
        out_specs=(
            pl.BlockSpec((tokens, tile), lambda i: (0, jnp.minimum(i, last_q))),
            pl.BlockSpec((tokens, tile), lambda i: (0, 0)),
        ),
        scratch_shapes=[pltpu.VMEM((tokens, width), bf16)],
    )


def head_rows(block, g):
    return jnp.concatenate(
        [
            block[:, (g * GROUP + j) * HEAD_DIM : (g * GROUP + j + 1) * HEAD_DIM]
            for j in range(GROUP)
        ],
        axis=0,
    )


def head_columns(rows, tokens):
    return [rows[j * tokens : (j + 1) * tokens] for j in range(GROUP)]


def key_rows(ref, seq, reps, tokens, column):
    columns = slice(column * HEAD_DIM, (column + 1) * HEAD_DIM)
    if reps == 1:
        return ref[:, columns]
    stride = reps * tokens
    return jnp.concatenate(
        [
            ref[a * stride + seq * tokens : a * stride + (seq + 1) * tokens, columns]
            for a in range(ref.shape[0] // stride)
        ],
        axis=0,
    )


def masked_scores(q, key_block, mask, tokens):
    scores = dot_nt(q, key_block) * SCALE
    keys = scores.shape[1]
    return (scores.reshape(GROUP, tokens, keys) + mask[None]).reshape(GROUP * tokens, keys)


def attend_kernel(pieces, reps, *refs):
    q_ref, x_ref, mask_ref, ow_ref, gain_ref = refs[:5]
    kv_refs = refs[5 : 5 + pieces]
    att_ref, hid_ref, n2_ref = refs[5 + pieces :]
    tokens = q_ref.shape[0] // reps
    for seq in range(reps):
        rows = slice(seq * tokens, (seq + 1) * tokens)
        q_all = q_ref[rows, :]
        for g in range(KV_HEADS):
            q = head_rows(q_all, g)
            scores = [
                masked_scores(q, key_rows(kv, seq, reps, tokens, g), mask_ref[p], tokens)
                for p, kv in enumerate(kv_refs)
            ]
            top = functools.reduce(
                jnp.maximum, [jnp.max(s, axis=-1, keepdims=True) for s in scores]
            )
            total = jnp.zeros_like(top)
            acc = jnp.zeros((GROUP * tokens, HEAD_DIM), f32)
            for s, kv in zip(scores, kv_refs):
                weights = jnp.exp(s - top)
                total = total + jnp.sum(weights, axis=-1, keepdims=True)
                acc = acc + dot_nn(
                    weights.astype(bf16), key_rows(kv, seq, reps, tokens, KV_HEADS + g)
                )
            low = (acc / total).astype(bf16)
            for j, block in enumerate(head_columns(low, tokens)):
                head = g * GROUP + j
                att_ref[rows, head * HEAD_DIM : (head + 1) * HEAD_DIM] = block
    hidden = x_ref[...].astype(f32) + dot_nn(att_ref[...], ow_ref[...])
    hid_ref[...] = hidden
    n2_ref[...] = (hidden * inverse_rms(hidden) * gain_ref[...].astype(f32)).astype(bf16)


def attend(q, x, mask, ow, gain, kv_pieces, reps):
    tokens, width = x.shape
    keys = sum(p.shape[0] for p in kv_pieces)
    return call(
        functools.partial(attend_kernel, len(kv_pieces), reps),
        (
            jax.ShapeDtypeStruct((tokens, QCOLS), bf16),
            jax.ShapeDtypeStruct((tokens, width), f32),
            jax.ShapeDtypeStruct((tokens, width), bf16),
        ),
        (q, x, mask, ow, gain, *kv_pieces),
        2 * tokens * QCOLS * width + 12 * tokens * QCOLS * keys // reps,
        2 * QCOLS * width + 4 * keys * KCOLS,
        "attend",
    )


def fill(scratch, refs):
    size = refs[0].shape[0]
    for p, ref in enumerate(refs):
        scratch[p * size : (p + 1) * size, :] = ref[...]


def mlp_kernel(pieces, *refs):
    n_refs = refs[:pieces]
    gate_ref, up_ref, down_ref = refs[pieces : pieces + 3]
    out_refs = refs[pieces + 3 : 2 * pieces + 3]
    cat_ref, acc_ref = refs[2 * pieces + 3 :]
    step = pl.program_id(0)

    @pl.when(step == 0)
    def _():
        fill(cat_ref, n_refs)
        acc_ref[...] = jnp.zeros_like(acc_ref)

    rows = cat_ref[...]
    gate_pre = dot_nt(rows, gate_ref[...])
    up_pre = dot_nt(rows, up_ref[...])
    activated = (jax.nn.sigmoid(gate_pre) * gate_pre * up_pre).astype(bf16)
    acc_ref[...] += dot_nn(activated, down_ref[...])

    @pl.when(step == pl.num_programs(0) - 1)
    def _():
        size = out_refs[0].shape[0]
        for p, ref in enumerate(out_refs):
            ref[...] = acc_ref[p * size : (p + 1) * size, :].astype(bf16)


def unit_tile(units, most):
    best = max(t for t in range(16, most + 1, 16) if units % t == 0)
    return best


def mlp(n_pieces, gate, up, down):
    units, width = gate.shape
    tokens = n_pieces[0].shape[0]
    count = len(n_pieces)
    tile = unit_tile(units, 512)
    whole = pl.BlockSpec((tokens, width), lambda i: (0, 0))
    part = pl.BlockSpec((tile, width), lambda i: (i, 0))
    return call(
        functools.partial(mlp_kernel, count),
        tuple(jax.ShapeDtypeStruct((tokens, width), bf16) for _ in n_pieces),
        (*n_pieces, gate, up, down),
        6 * count * tokens * width * units,
        6 * width * units,
        "mlp",
        grid=(units // tile,),
        in_specs=[whole] * count + [part] * 3,
        out_specs=tuple(whole for _ in n_pieces),
        scratch_shapes=[
            pltpu.VMEM((count * tokens, width), bf16),
            pltpu.VMEM((count * tokens, width), f32),
        ],
    )


def swiglu_backward(gate_pre, up_pre, grad_act):
    sigmoid = jax.nn.sigmoid(gate_pre)
    silu = gate_pre * sigmoid
    grad_gate = (grad_act * up_pre * (sigmoid + silu * (1.0 - sigmoid))).astype(bf16)
    grad_up = (grad_act * silu).astype(bf16)
    return silu, grad_gate, grad_up


def mlp_back_kernel(pieces, *refs):
    n_refs = refs[:pieces]
    g_refs = refs[pieces : 2 * pieces]
    gate_ref, up_ref, down_ref = refs[2 * pieces : 2 * pieces + 3]
    out_refs = refs[2 * pieces + 3 : 3 * pieces + 3]
    cat_ref, gcat_ref, acc_ref = refs[3 * pieces + 3 :]
    step = pl.program_id(0)

    @pl.when(step == 0)
    def _():
        fill(cat_ref, n_refs)
        fill(gcat_ref, g_refs)
        acc_ref[...] = jnp.zeros_like(acc_ref)

    rows = cat_ref[...]
    gate_pre = dot_nt(rows, gate_ref[...])
    up_pre = dot_nt(rows, up_ref[...])
    grad_act = dot_nt(gcat_ref[...], down_ref[...])
    _, grad_gate, grad_up = swiglu_backward(gate_pre, up_pre, grad_act)
    acc_ref[...] += dot_nn(grad_gate, gate_ref[...]) + dot_nn(grad_up, up_ref[...])

    @pl.when(step == pl.num_programs(0) - 1)
    def _():
        size = out_refs[0].shape[0]
        for p, ref in enumerate(out_refs):
            ref[...] = acc_ref[p * size : (p + 1) * size, :].astype(bf16)


def mlp_back(n_pieces, g_pieces, gate, up, down):
    units, width = gate.shape
    tokens = n_pieces[0].shape[0]
    count = len(n_pieces)
    tile = unit_tile(units, 512)
    whole = pl.BlockSpec((tokens, width), lambda i: (0, 0))
    part = pl.BlockSpec((tile, width), lambda i: (i, 0))
    return call(
        functools.partial(mlp_back_kernel, count),
        tuple(jax.ShapeDtypeStruct((tokens, width), bf16) for _ in n_pieces),
        (*n_pieces, *g_pieces, gate, up, down),
        10 * count * tokens * width * units,
        6 * width * units,
        "mlp_back",
        grid=(units // tile,),
        in_specs=[whole] * (2 * count) + [part] * 3,
        out_specs=tuple(whole for _ in n_pieces),
        scratch_shapes=[
            pltpu.VMEM((count * tokens, width), bf16),
            pltpu.VMEM((count * tokens, width), bf16),
            pltpu.VMEM((count * tokens, width), f32),
        ],
    )


def sum_refs(refs):
    total = refs[0][...].astype(f32)
    for ref in refs[1:]:
        total = total + ref[...].astype(f32)
    return total


def attend_back_kernel(pieces, terms, reps, *refs):
    gy_ref, hid_ref, gain_ref, ow_ref, q_ref, mask_ref, cos_ref, sin_ref = refs[:8]
    kv_refs = refs[8 : 8 + pieces]
    t_refs = refs[8 + pieces : 8 + pieces + terms]
    gh_ref, ghl_ref, dq_ref, mg_ref = refs[8 + pieces + terms : 12 + pieces + terms]
    dkv_refs = refs[12 + pieces + terms :]
    tokens = q_ref.shape[0] // reps
    grad_from_two, grad_gain = norm_backward(
        sum_refs(t_refs), hid_ref[...], gain_ref[...].astype(f32)
    )
    mg_ref[...] = grad_gain
    grad_hidden = gy_ref[...].astype(f32) + grad_from_two
    gh_ref[...] = grad_hidden
    grad_low = grad_hidden.astype(bf16)
    ghl_ref[...] = grad_low
    grad_att = dot_nt(grad_low, ow_ref[...]).astype(bf16)
    cos = cos_ref[...]
    sin = sin_ref[...]
    for seq in range(reps):
        rows = slice(seq * tokens, (seq + 1) * tokens)
        q_all = q_ref[rows, :]
        grad_all = grad_att[rows, :]
        for g in range(KV_HEADS):
            q = head_rows(q_all, g)
            go = head_rows(grad_all, g)
            key_blocks = [key_rows(kv, seq, reps, tokens, g) for kv in kv_refs]
            scores = [
                masked_scores(q, k, mask_ref[p], tokens) for p, k in enumerate(key_blocks)
            ]
            top = functools.reduce(
                jnp.maximum, [jnp.max(s, axis=-1, keepdims=True) for s in scores]
            )
            weights = [jnp.exp(s - top) for s in scores]
            total = functools.reduce(
                jnp.add, [jnp.sum(w, axis=-1, keepdims=True) for w in weights]
            )
            scale = 1.0 / total
            probs = [w * scale for w in weights]
            grad_probs = [
                dot_nt(go, key_rows(kv, seq, reps, tokens, KV_HEADS + g)) for kv in kv_refs
            ]
            delta = functools.reduce(
                jnp.add,
                [jnp.sum(p * d, axis=-1, keepdims=True) for p, d in zip(probs, grad_probs)],
            )
            dq = jnp.zeros((GROUP * tokens, HEAD_DIM), f32)
            for p in range(pieces):
                grad_z = (probs[p] * (grad_probs[p] - delta) * SCALE).astype(bf16)
                dq = dq + dot_nn(grad_z, key_blocks[p])
                dk = dot_tn(grad_z, q).astype(bf16)
                dv = dot_tn(probs[p].astype(bf16), go).astype(bf16)
                stride = reps * tokens
                for a in range(dk.shape[0] // tokens):
                    here = slice(a * stride + seq * tokens, a * stride + (seq + 1) * tokens)
                    part = slice(a * tokens, (a + 1) * tokens)
                    dkv_refs[p][here, g * HEAD_DIM : (g + 1) * HEAD_DIM] = dk[part]
                    v_at = (KV_HEADS + g) * HEAD_DIM
                    dkv_refs[p][here, v_at : v_at + HEAD_DIM] = dv[part]
            for j, block in enumerate(head_columns(dq, tokens)):
                head = g * GROUP + j
                dq_ref[rows, head * HEAD_DIM : (head + 1) * HEAD_DIM] = turn(
                    block, cos, -sin
                ).astype(bf16)


def attend_back(gy, hidden, gain, ow, q, mask, cos, sin, kv_pieces, terms, reps):
    tokens, width = gy.shape
    keys = sum(p.shape[0] for p in kv_pieces)
    return call(
        functools.partial(attend_back_kernel, len(kv_pieces), len(terms), reps),
        (
            jax.ShapeDtypeStruct((tokens, width), f32),
            jax.ShapeDtypeStruct((tokens, width), bf16),
            jax.ShapeDtypeStruct((tokens, QCOLS), bf16),
            jax.ShapeDtypeStruct((1, width), f32),
            *(jax.ShapeDtypeStruct(p.shape, bf16) for p in kv_pieces),
        ),
        (gy, hidden, gain, ow, q, mask, cos, sin, *kv_pieces, *terms),
        2 * tokens * QCOLS * width + 30 * tokens * QCOLS * keys // reps,
        2 * QCOLS * width + 8 * keys * KCOLS,
        "attend_back",
        limit=56,
    )


def project_back_kernel(terms, reps, *refs):
    dq_ref, x_ref, gh_ref, gain_ref, w_ref, cos_ref, sin_ref = refs[:7]
    t_refs = refs[7 : 7 + terms]
    gin_ref, gp_ref, n_ref, b_ref, ag_ref = refs[7 + terms :]
    dkv = sum_refs(t_refs)
    cos = repeat_rows(cos_ref[...], reps)
    sin = repeat_rows(sin_ref[...], reps)
    parts = [
        turn(dkv[:, j * HEAD_DIM : (j + 1) * HEAD_DIM], cos, -sin) for j in range(KV_HEADS)
    ]
    parts.append(dkv[:, KCOLS:])
    gp_ref[:, :QCOLS] = dq_ref[...]
    gp_ref[:, QCOLS:] = jnp.concatenate(parts, axis=1).astype(bf16)
    grad_projected = gp_ref[...]
    b_ref[...] = jnp.sum(grad_projected.astype(f32), axis=0, keepdims=True)
    x = x_ref[...].astype(f32)
    gain = gain_ref[...].astype(f32)
    n_ref[...] = (x * inverse_rms(x) * gain).astype(bf16)
    grad_normed = dot_nt(grad_projected, w_ref[...])
    grad_source, grad_gain = norm_backward(grad_normed, x, gain)
    ag_ref[...] = grad_gain
    gin_ref[...] = (gh_ref[...] + grad_source).astype(bf16)


def project_back(dq, x, gh, gain, w, cos, sin, terms, reps):
    tokens, width = x.shape
    columns = w.shape[1]
    return call(
        functools.partial(project_back_kernel, len(terms), reps),
        (
            jax.ShapeDtypeStruct((tokens, width), bf16),
            jax.ShapeDtypeStruct((tokens, columns), bf16),
            jax.ShapeDtypeStruct((tokens, width), bf16),
            jax.ShapeDtypeStruct((1, columns), f32),
            jax.ShapeDtypeStruct((1, width), f32),
        ),
        (dq, x, gh, gain, w, cos, sin, *terms),
        2 * tokens * width * columns,
        2 * width * columns,
        "project_back",
    )


def weight_grad_kernel(aliased, *refs):
    n_ref, g_ref, gate_ref, up_ref, down_ref = refs[:5]
    dg_ref, du_ref, dd_ref = refs[5 + aliased :]
    step = pl.program_id(1)

    @pl.when(step == 0)
    def _():
        dg_ref[...] = jnp.zeros_like(dg_ref)
        du_ref[...] = jnp.zeros_like(du_ref)
        dd_ref[...] = jnp.zeros_like(dd_ref)

    rows = n_ref[...]
    grads = g_ref[...]
    gate_pre = dot_nt(gate_ref[...], rows)
    up_pre = dot_nt(up_ref[...], rows)
    grad_act = dot_nt(down_ref[...], grads)
    silu, grad_gate, grad_up = swiglu_backward(gate_pre, up_pre, grad_act)
    activated = (silu * up_pre).astype(bf16)
    dg_ref[...] += dot_nn(grad_gate, rows)
    du_ref[...] += dot_nn(grad_up, rows)
    dd_ref[...] += dot_nn(activated, grads)


def weight_grads(n_all, g_all, gate, up, down, calls):
    units, width = gate.shape
    tokens = n_all.shape[0]
    tile = unit_tile(units, 320)
    chunk = math.gcd(tokens, 1024)
    tiles = units // tile
    shape = jax.ShapeDtypeStruct((units, width), f32)
    outs = ()
    first = 0
    for index in range(calls):
        here = tiles // calls + (1 if index < tiles % calls else 0)
        part = pl.BlockSpec((tile, width), lambda i, j, first=first: (i + first, 0))
        rows = pl.BlockSpec((chunk, width), lambda i, j: (j, 0))
        outs = call(
            functools.partial(weight_grad_kernel, len(outs)),
            (shape,) * 3,
            (n_all, g_all, gate, up, down, *outs),
            12 * tokens * width * tile * here,
            18 * width * tile * here,
            "weight_grads",
            limit=56,
            grid=(here, tokens // chunk),
            in_specs=[rows] * 2 + [part] * 3 + [pl.BlockSpec(memory_space=pl.ANY)] * len(outs),
            out_specs=(part,) * 3,
            input_output_aliases={5 + k: k for k in range(len(outs))},
        )
        first += here
    return outs


def body(
    inputs,
    cotangent,
    attn_gain,
    qkv_weight,
    qkv_bias,
    out_weight,
    mlp_gain,
    gate_weight,
    up_weight,
    down_weight,
):
    first = lax.axis_index("section") == 0
    micro, rows_here, _, width = inputs.shape
    fsdp = lax.axis_size("fsdp")
    ctx = lax.axis_size("ctx")
    fsdp_at = lax.axis_index("fsdp")
    ctx_at = lax.axis_index("ctx")
    tokens = 2 * rows_here
    reps = MICROS
    chunks = micro // reps
    steps = chunks + LAG
    span_rows = rows_here * fsdp
    half_rows = span_rows * ctx

    def places_of(c, f):
        index = (c * fsdp + f) * rows_here + jnp.arange(rows_here, dtype=jnp.int32)
        return storage_place(index, span_rows, half_rows).reshape(tokens)

    own = places_of(ctx_at, fsdp_at)
    key_places = jnp.stack(
        [
            jnp.concatenate([places_of(ctx_at ^ a, fsdp_at ^ r) for a in range(ctx)])
            for r in relative_order(fsdp)
        ]
    )
    mask = jnp.where(key_places[:, None, :] <= own[None, :, None], 0.0, NEGATIVE).astype(f32)
    half = HEAD_DIM // 2
    frequency = ROPE_BASE ** (-(jnp.arange(half, dtype=f32) * 2.0) / HEAD_DIM)
    angles = own.astype(f32)[:, None] * frequency
    cos = jnp.concatenate([jnp.cos(angles)] * 2, axis=1)
    sin = jnp.concatenate([-jnp.sin(angles), jnp.sin(angles)], axis=1)

    def gathered(shard):
        return lax.all_gather(shard, "fsdp", axis=0, tiled=True)

    qkv_full = gathered(qkv_weight[0])
    attn_full = gathered(attn_gain[0])[None]
    bias_full = gathered(qkv_bias[0])[None]
    mlp_full = gathered(mlp_gain[0])[None]
    out_full = gathered(out_weight[0])
    gate, up, down = gate_weight[0], up_weight[0], down_weight[0]

    def chunked(array):
        return array.reshape(chunks, reps * tokens, width)

    in_chunks = chunked(inputs)
    cot_chunks = chunked(cotangent)

    outputs, saved, moved = [], [], []
    for t in range(steps):
        if t < LAG:
            x = in_chunks[t]
        else:
            x = jnp.where(first, in_chunks[min(t, chunks - 1)], moved[t - LAG])
        q, kv = project(x, attn_full, qkv_full, bias_full, cos, sin, reps)
        kv_ctx = jnp.concatenate([kv] + [exchange(kv, "ctx", a) for a in range(1, ctx)], axis=0)
        kv_pieces = gather_pieces(kv_ctx, "fsdp")
        attended, hidden, n2 = attend(q, x, mask, out_full, mlp_full, kv_pieces, reps)
        n2_pieces = gather_pieces(n2, "fsdp")
        parts = mlp(n2_pieces, gate, up, down)
        terms = reduce_pieces(list(parts), "fsdp")
        y = add_low([hidden] + terms)
        outputs.append(y)
        if t < chunks:
            moved.append(passed_along(y, "section", 1))
        saved.append((x, q, attended, hidden, *kv_pieces, *n2_pieces))

    def pick(early, late):
        return jnp.where(first, early, late)

    n2_own = jnp.concatenate(
        [pick(saved[m][4 + fsdp], saved[m + LAG][4 + fsdp]) for m in range(chunks)], axis=0
    )
    n2_all = lax.all_gather(n2_own, ("ctx", "fsdp"), axis=0, tiled=True)

    grads_in, grads_moved, gys, smalls, factors = [], [], [], [], []
    for u in range(steps):
        if u < LAG:
            gy = jnp.where(first, jnp.zeros_like(cot_chunks[u]), cot_chunks[u])
        elif u < chunks:
            gy = pick(grads_moved[u - LAG], cot_chunks[u])
        else:
            gy = pick(grads_moved[u - LAG], jnp.zeros_like(cot_chunks[0]))
        gys.append(gy)
        both = zip(saved[max(u - LAG, 0)], saved[min(u + LAG, steps - 1)])
        x, q, attended, hidden, *rest = [pick(early, late) for early, late in both]
        kv_pieces, n2_pieces = rest[:fsdp], rest[fsdp:]
        g_pieces = gather_pieces(gy, "fsdp")
        parts = mlp_back(n2_pieces, g_pieces, gate, up, down)
        terms = reduce_pieces(list(parts), "fsdp")
        gh, gh_low, dq, grad_mlp_gain, *dkv = attend_back(
            gy, hidden, mlp_full, out_full, q, mask, cos, sin, kv_pieces, terms, reps
        )
        dkv_ctx = add_low(reduce_pieces(dkv, "fsdp"))
        size = reps * tokens
        dkv_terms = [
            dkv_ctx[a * size : (a + 1) * size]
            if a == 0
            else exchange(dkv_ctx[a * size : (a + 1) * size], "ctx", a)
            for a in range(ctx)
        ]
        g_in, g_proj, normed, grad_bias, grad_attn_gain = project_back(
            dq, x, gh, attn_full, qkv_full, cos, sin, dkv_terms, reps
        )
        grads_in.append(g_in)
        if u < chunks:
            grads_moved.append(passed_along(g_in, "section", -1))
        smalls.append(jnp.concatenate([grad_attn_gain, grad_bias, grad_mlp_gain], axis=1))
        factors.append((normed, g_proj, attended, gh_low))

    g_own = jnp.concatenate([pick(gys[m + LAG], gys[m]) for m in range(chunks)], axis=0)
    g_all = lax.all_gather(g_own, ("ctx", "fsdp"), axis=0, tiled=True)
    grad_gate, grad_up, grad_down = weight_grads(n2_all, g_all, gate, up, down, 4)

    normed_all, proj_all, attended_all, gh_all = (
        jnp.concatenate([pick(factors[m + LAG][k], factors[m][k]) for m in range(chunks)], axis=0)
        for k in range(4)
    )

    def own_shard(whole):
        shard = lax.psum_scatter(whole.astype(bf16), "fsdp", scatter_dimension=0, tiled=True)
        return lax.psum(shard, "ctx").astype(f32)

    grad_qkv = own_shard(dot_tn(normed_all, proj_all))
    grad_out = own_shard(dot_tn(attended_all, gh_all))

    small = lax.psum(functools.reduce(jnp.add, smalls)[0], ("ctx", "fsdp"))

    def cut(start, length):
        part = length // fsdp
        return lax.dynamic_slice(small, (start + fsdp_at * part,), (part,))

    lead = QCOLS + KCOLS
    columns = QCOLS + 2 * KCOLS
    grad_attn_gain = cut(0, width)
    grad_bias_lead = cut(width, lead)
    grad_bias_value = cut(width + lead, columns - lead)
    grad_mlp_gain = cut(width + columns, width)

    def restore(parts):
        return jnp.stack(parts).reshape(inputs.shape)

    layer_outputs = restore([pick(outputs[m], outputs[m + LAG]) for m in range(chunks)])
    input_grads = restore([pick(grads_in[m + LAG], grads_in[m]) for m in range(chunks)])
    return (
        layer_outputs[None],
        input_grads[None],
        grad_attn_gain[None],
        grad_qkv[None],
        grad_bias_lead[None],
        grad_bias_value[None],
        grad_out[None],
        grad_mlp_gain[None],
        grad_gate[None],
        grad_up[None],
        grad_down[None],
    )


def solution(mesh):
    rows = P(None, ("ctx", "fsdp"), None, None)
    vector = P("section", "fsdp")
    matrix = P("section", "fsdp", None)
    stacked = P("section", None, ("ctx", "fsdp"), None, None)
    in_specs = (rows, rows, vector, matrix, vector, matrix, vector, matrix, matrix, matrix)
    out_specs = (
        stacked,
        stacked,
        vector,
        matrix,
        vector,
        vector,
        matrix,
        vector,
        matrix,
        matrix,
        matrix,
    )
    return jax.shard_map(body, mesh=mesh, in_specs=in_specs, out_specs=out_specs, check_vma=False)
```

```python
import functools
import math

import jax
import jax.numpy as jnp
from jax import lax
from jax.experimental import pallas as pl
from jax.experimental.pallas import tpu as pltpu
from jax.sharding import PartitionSpec as P

HEADS = 12
KV_HEADS = 2
HEAD_DIM = 128
GROUP = HEADS // KV_HEADS
EPS = 1e-06
ROPE_BASE = 1000000.0
NEGATIVE = -1e30
QCOLS = HEADS * HEAD_DIM
KCOLS = KV_HEADS * HEAD_DIM
SCALE = HEAD_DIM ** (-0.5)

MICROS = 1
LAG = 2
UNITS = 512

f32 = jnp.float32
bf16 = jnp.bfloat16
MIB = 1 << 20


def dot_nn(a, b):
    return lax.dot_general(a, b, (((1,), (0,)), ((), ())), preferred_element_type=f32)


def dot_nt(a, b):
    return lax.dot_general(a, b, (((1,), (1,)), ((), ())), preferred_element_type=f32)


def dot_tn(a, b):
    return lax.dot_general(a, b, (((0,), (0,)), ((), ())), preferred_element_type=f32)


def inverse_rms(values):
    return lax.rsqrt(jnp.mean(values * values, axis=-1, keepdims=True) + EPS)


def norm_backward(grad_normed, values, gain):
    inverse = inverse_rms(values)
    scaled = grad_normed * gain
    grad_values = inverse * scaled - values * (
        inverse**3 * jnp.mean(scaled * values, axis=-1, keepdims=True)
    )
    grad_gain = jnp.sum(grad_normed * values * inverse, axis=0, keepdims=True)
    return grad_values, grad_gain


def storage_place(indices, span_rows, half_rows):
    second = 2 * half_rows - span_rows * (indices // span_rows + 1) + indices % span_rows
    return jnp.stack([indices, second], axis=-1)


def exchange(block, axis, mask):
    size = lax.axis_size(axis)
    return lax.ppermute(block, axis, [(i, i ^ mask) for i in range(size)])


def passed_along(block, axis, distance):
    devices = range(lax.axis_size(axis))
    route = [(i - distance, i) for i in devices if i - distance in devices]
    return lax.ppermute(block, axis, route)


def bits_of(size):
    return [1 << b for b in reversed(range(size.bit_length() - 1))]


def relative_order(size):
    order = [0]
    for bit in bits_of(size):
        order = order + [r ^ bit for r in order]
    return order


def gather_pieces(block, axis):
    pieces = [block]
    for bit in bits_of(lax.axis_size(axis)):
        pieces = pieces + [exchange(p, axis, bit) for p in pieces]
    return pieces


def add_low(terms):
    total = terms[0].astype(f32)
    for term in terms[1:]:
        total = total + term.astype(f32)
    return total.astype(bf16)


def reduce_pieces(parts, axis):
    terms = [[p] for p in parts]
    for bit in reversed(bits_of(lax.axis_size(axis))):
        half = len(terms) // 2
        sent = [t[0] if len(t) == 1 else add_low(t) for t in terms[half:]]
        terms = [t + [exchange(s, axis, bit)] for t, s in zip(terms[:half], sent)]
    return terms[0]


def call(kernel, out_shape, args, flops, moved, name, limit=24, **kwargs):
    return pl.pallas_call(
        kernel,
        out_shape=out_shape,
        compiler_params=pltpu.CompilerParams(vmem_limit_bytes=limit * MIB),
        cost_estimate=pl.CostEstimate(flops=flops, bytes_accessed=moved, transcendentals=0),
        name=name,
        **kwargs,
    )(*args)


ANY = pl.BlockSpec(memory_space=pl.ANY)
VMEM = pl.BlockSpec(memory_space=pltpu.VMEM)
SMEM = pl.BlockSpec(memory_space=pltpu.SMEM)


def hold_kernel(count, *refs):
    copies = [
        pltpu.make_async_copy(refs[k], refs[count + k], refs[-1].at[k]) for k in range(count)
    ]
    for copy in copies:
        copy.start()
    for copy in copies:
        copy.wait()


def hold(*arrays):
    return call(
        functools.partial(hold_kernel, len(arrays)),
        tuple(pltpu.VMEM(a.shape, a.dtype) for a in arrays),
        [far(a) for a in arrays],
        0,
        2 * sum(a.size for a in arrays),
        "hold",
        limit=4,
        in_specs=[ANY] * len(arrays),
        out_specs=tuple(VMEM for _ in arrays),
        scratch_shapes=[pltpu.SemaphoreType.DMA((len(arrays),))],
    )


def held(array):
    return pltpu.with_memory_space_constraint(array, pltpu.VMEM)


def far(array):
    return pltpu.with_memory_space_constraint(array, pltpu.HBM)


def bring(flag_ref, sources, targets, sem):
    copies = []
    for k, (source, target) in enumerate(zip(sources, targets)):
        if len(source) == 1:
            copy = pltpu.make_async_copy(source[0], target, sem.at[k])
            copy.start()
        else:
            for is_first, ref in zip((1, 0), source):
                copy = pltpu.make_async_copy(ref, target, sem.at[k])
                pl.when(flag_ref[0] == is_first)(copy.start)
        copies.append(copy)
    return copies


def taken(refs, counts):
    groups = []
    for count in counts:
        groups.append(refs[:count])
        refs = refs[count:]
    return groups, refs


def turn(value, cos, sin):
    return value * cos + pltpu.roll(value, HEAD_DIM // 2, 1) * sin


def repeat_rows(table, count):
    return table if count == 1 else jnp.concatenate([table] * count, axis=0)


def choose(flag_ref, refs):
    if len(refs) == 1:
        return refs[0][...]
    return jnp.where(flag_ref[0] == 1, refs[0][...], refs[1][...])


def column_copies(source, target, sem):
    tile = 2 * KCOLS
    copies = []
    for k in range(source.shape[1] // tile):
        here = (slice(None), pl.ds(k * tile, tile))
        copies.append(pltpu.make_async_copy(source.at[here], target.at[here], sem.at[k]))
        copies[-1].start()
    return copies


def project_kernel(reps, versions, *refs):
    flag_ref, gain_ref, w_hbm, b_ref, cos_ref, sin_ref = refs[:6]
    x_refs = refs[6 : 6 + versions]
    q_ref, kv_ref, n_ref, w_ref, sem = refs[-5:]
    copies = column_copies(w_hbm, w_ref, sem)
    x = choose(flag_ref, x_refs).astype(f32)
    n_ref[...] = (x * inverse_rms(x) * gain_ref[...].astype(f32)).astype(bf16)
    cos = repeat_rows(cos_ref[...], reps)
    sin = repeat_rows(sin_ref[...], reps)
    tile = 2 * KCOLS
    for start in range(0, w_ref.shape[1], tile):
        here = slice(start, start + tile)
        copies[start // tile].wait()
        projected = dot_nn(n_ref[...], w_ref[:, here]) + b_ref[:, here].astype(f32)
        turned = []
        for j in range(0, tile, HEAD_DIM):
            part = projected[:, j : j + HEAD_DIM]
            turned.append(part if start + j >= QCOLS + KCOLS else turn(part, cos, sin))
        low = jnp.concatenate(turned, axis=1).astype(bf16)
        if start < QCOLS:
            q_ref[:, here] = low
        else:
            kv_ref[...] = low


def project(flag, xs, gain, w, b, cos, sin, reps, after=()):
    tokens, width = xs[0].shape
    columns = w.shape[1]
    return call(
        functools.partial(project_kernel, reps, len(xs)),
        (
            jax.ShapeDtypeStruct((tokens, QCOLS), bf16),
            jax.ShapeDtypeStruct((tokens, 2 * KCOLS), bf16),
        ),
        (flag, gain, far(w), b, cos, sin, *xs, *after),
        2 * tokens * width * columns,
        2 * width * columns,
        "project",
        limit=16,
        in_specs=[SMEM, VMEM, ANY] + [VMEM] * (3 + len(xs)) + [ANY] * len(after),
        out_specs=(VMEM, VMEM),
        scratch_shapes=[
            pltpu.VMEM((tokens, width), bf16),
            pltpu.VMEM((width, columns), bf16),
            pltpu.SemaphoreType.DMA((columns // (2 * KCOLS),)),
        ],
    )


def head_rows(block, g):
    return jnp.concatenate(
        [
            block[:, (g * GROUP + j) * HEAD_DIM : (g * GROUP + j + 1) * HEAD_DIM]
            for j in range(GROUP)
        ],
        axis=0,
    )


def head_columns(rows, tokens):
    return [rows[j * tokens : (j + 1) * tokens] for j in range(GROUP)]


def key_rows(ref, seq, reps, tokens, column):
    columns = slice(column * HEAD_DIM, (column + 1) * HEAD_DIM)
    if reps == 1:
        return ref[:, columns]
    stride = reps * tokens
    return jnp.concatenate(
        [
            ref[a * stride + seq * tokens : a * stride + (seq + 1) * tokens, columns]
            for a in range(ref.shape[0] // stride)
        ],
        axis=0,
    )


def masked_scores(q, key_block, mask, tokens):
    scores = dot_nt(q, key_block) * SCALE
    keys = scores.shape[1]
    return (scores.reshape(GROUP, tokens, keys) + mask[None]).reshape(GROUP * tokens, keys)


def attend_kernel(pieces, reps, versions, *refs):
    flag_ref, q_ref, mask_ref, ow_hbm, gain_ref = refs[:5]
    kv_refs = refs[5 : 5 + pieces]
    x_refs = refs[5 + pieces : 5 + pieces + versions]
    att_ref, hid_ref, n2_ref, ow_ref, sem = refs[5 + pieces + versions :]
    weights_in = pltpu.make_async_copy(ow_hbm, ow_ref, sem)
    weights_in.start()
    tokens = q_ref.shape[0] // reps
    for seq in range(reps):
        rows = slice(seq * tokens, (seq + 1) * tokens)
        q_all = q_ref[rows, :]
        for g in range(KV_HEADS):
            q = head_rows(q_all, g)
            scores = [
                masked_scores(q, key_rows(kv, seq, reps, tokens, g), mask_ref[p], tokens)
                for p, kv in enumerate(kv_refs)
            ]
            top = functools.reduce(
                jnp.maximum, [jnp.max(s, axis=-1, keepdims=True) for s in scores]
            )
            total = jnp.zeros_like(top)
            acc = jnp.zeros((GROUP * tokens, HEAD_DIM), f32)
            for s, kv in zip(scores, kv_refs):
                weights = jnp.exp(s - top)
                total = total + jnp.sum(weights, axis=-1, keepdims=True)
                acc = acc + dot_nn(
                    weights.astype(bf16), key_rows(kv, seq, reps, tokens, KV_HEADS + g)
                )
            low = (acc / total).astype(bf16)
            for j, block in enumerate(head_columns(low, tokens)):
                head = g * GROUP + j
                att_ref[rows, head * HEAD_DIM : (head + 1) * HEAD_DIM] = block
    weights_in.wait()
    hidden = choose(flag_ref, x_refs).astype(f32) + dot_nn(att_ref[...], ow_ref[...])
    hid_ref[...] = hidden
    n2_ref[...] = (hidden * inverse_rms(hidden) * gain_ref[...].astype(f32)).astype(bf16)


def attend(flag, q, xs, mask, ow, gain, kv_pieces, reps):
    tokens, width = xs[0].shape
    keys = sum(p.shape[0] for p in kv_pieces)
    return call(
        functools.partial(attend_kernel, len(kv_pieces), reps, len(xs)),
        (
            jax.ShapeDtypeStruct((tokens, QCOLS), bf16),
            jax.ShapeDtypeStruct((tokens, width), f32),
            jax.ShapeDtypeStruct((tokens, width), bf16),
        ),
        (flag, q, mask, far(ow), gain, *kv_pieces, *xs),
        2 * tokens * QCOLS * width + 12 * tokens * QCOLS * keys // reps,
        4 * keys * KCOLS + 12 * tokens * width,
        "attend",
        limit=16 + 24 * keys // (reps * 4096),
        in_specs=[SMEM, VMEM, VMEM, ANY] + [VMEM] * (1 + len(kv_pieces) + len(xs)),
        out_specs=(VMEM,) * 3,
        scratch_shapes=[pltpu.VMEM(ow.shape, bf16), pltpu.SemaphoreType.DMA(())],
    )


def fill(scratch, refs):
    size = refs[0].shape[0]
    for p, ref in enumerate(refs):
        scratch[p * size : (p + 1) * size, :] = ref[...]


def spread(out_refs, acc_ref):
    size = out_refs[0].shape[0]
    for p, ref in enumerate(out_refs):
        ref[...] = acc_ref[p * size : (p + 1) * size, :].astype(bf16)


def unit_spans(units):
    return [slice(at, min(at + UNITS, units)) for at in range(0, units, UNITS)]


def mlp_kernel(pieces, *refs):
    n_refs = refs[:pieces]
    gate_ref, up_ref, down_ref = refs[pieces : pieces + 3]
    out_refs = refs[-pieces - 2 : -2]
    cat_ref, acc_ref = refs[-2:]
    fill(cat_ref, n_refs)
    for k, here in enumerate(unit_spans(gate_ref.shape[0])):
        rows = cat_ref[...]
        gate_pre = dot_nt(rows, gate_ref[here, :])
        up_pre = dot_nt(rows, up_ref[here, :])
        activated = (jax.nn.sigmoid(gate_pre) * gate_pre * up_pre).astype(bf16)
        term = dot_nn(activated, down_ref[here, :])
        if k == 0:
            acc_ref[...] = term
        else:
            acc_ref[...] += term
    spread(out_refs, acc_ref)


def mlp(n_pieces, gate, up, down, after=()):
    units, width = gate.shape
    tokens = n_pieces[0].shape[0]
    count = len(n_pieces)
    return call(
        functools.partial(mlp_kernel, count),
        tuple(jax.ShapeDtypeStruct((tokens, width), bf16) for _ in n_pieces),
        (*n_pieces, held(gate), held(up), held(down), *after),
        6 * count * tokens * width * units,
        4 * count * tokens * width,
        "mlp",
        limit=12,
        in_specs=[VMEM] * (count + 3) + [ANY] * len(after),
        out_specs=(VMEM,) * count,
        scratch_shapes=[
            pltpu.VMEM((count * tokens, width), bf16),
            pltpu.VMEM((count * tokens, width), f32),
        ],
    )


def swiglu_backward(gate_pre, up_pre, grad_act):
    sigmoid = jax.nn.sigmoid(gate_pre)
    silu = gate_pre * sigmoid
    grad_gate = (grad_act * up_pre * (sigmoid + silu * (1.0 - sigmoid))).astype(bf16)
    grad_up = (grad_act * silu).astype(bf16)
    return silu, grad_gate, grad_up


def mlp_back_kernel(pieces, versions, *refs):
    (flags, weights, n_refs, g_refs), rest = taken(
        refs, (1, 3, pieces * versions, pieces)
    )
    gate_ref, up_ref, down_ref = weights
    out_refs = rest[-pieces - 4 : -4]
    cat_ref, gcat_ref, acc_ref, sem = rest[-4:]
    size = cat_ref.shape[0] // pieces
    spans = [pl.ds(p * size, size) for p in range(pieces)]
    sources = [n_refs[p * versions : (p + 1) * versions] for p in range(pieces)]
    copies = bring(
        flags[0],
        sources + [(g,) for g in g_refs],
        [cat_ref.at[span] for span in spans] + [gcat_ref.at[span] for span in spans],
        sem,
    )
    for copy in copies:
        copy.wait()
    for k, here in enumerate(unit_spans(gate_ref.shape[0])):
        rows = cat_ref[...]
        gate_pre = dot_nt(rows, gate_ref[here, :])
        up_pre = dot_nt(rows, up_ref[here, :])
        grad_act = dot_nt(gcat_ref[...], down_ref[here, :])
        _, grad_gate, grad_up = swiglu_backward(gate_pre, up_pre, grad_act)
        term = dot_nn(grad_gate, gate_ref[here, :]) + dot_nn(grad_up, up_ref[here, :])
        if k == 0:
            acc_ref[...] = term
        else:
            acc_ref[...] += term
    spread(out_refs, acc_ref)


def mlp_back(flag, n_versions, g_pieces, gate, up, down, after):
    units, width = gate.shape
    tokens = g_pieces[0].shape[0]
    count = len(g_pieces)
    versions = len(n_versions[0])
    n_arrays = [far(array) for piece in n_versions for array in piece]
    return call(
        functools.partial(mlp_back_kernel, count, versions),
        tuple(jax.ShapeDtypeStruct((tokens, width), bf16) for _ in g_pieces),
        (flag, held(gate), held(up), held(down), *n_arrays, *g_pieces, *after),
        10 * count * tokens * width * units,
        6 * count * tokens * width,
        "mlp_back",
        limit=16,
        in_specs=[SMEM] + [VMEM] * 3 + [ANY] * (len(n_arrays) + count + len(after)),
        out_specs=(VMEM,) * count,
        scratch_shapes=[
            pltpu.VMEM((count * tokens, width), bf16),
            pltpu.VMEM((count * tokens, width), bf16),
            pltpu.VMEM((count * tokens, width), f32),
            pltpu.SemaphoreType.DMA((2 * count,)),
        ],
    )


def sum_refs(refs):
    total = refs[0][...].astype(f32)
    for ref in refs[1:]:
        total = total + ref[...].astype(f32)
    return total


def attend_back_kernel(pieces, terms, reps, versions, *refs):
    (fixed, t_refs, sources, outs, dkv_refs, scratch), _ = taken(
        refs, (7, terms, (2 + pieces) * versions, 4, pieces, 6)
    )
    flag_ref, gy_ref, gain_ref, ow_hbm, mask_ref, cos_ref, sin_ref = fixed
    gh_ref, ghl_ref, dq_ref, mg_ref = outs
    hid_ref, q_ref, kv_ref, sem, ow_ref, ow_sem = scratch
    weights_in = pltpu.make_async_copy(ow_hbm, ow_ref, ow_sem)
    kv_refs = [kv_ref.at[p] for p in range(pieces)]
    copies = bring(
        flag_ref,
        [sources[k * versions : (k + 1) * versions] for k in range(2 + pieces)],
        [hid_ref, q_ref, *kv_refs],
        sem,
    )
    weights_in.start()
    tokens = q_ref.shape[0] // reps
    grad_normed = sum_refs(t_refs)
    for copy in copies:
        copy.wait()
    grad_from_two, grad_gain = norm_backward(
        grad_normed, hid_ref[...], gain_ref[...].astype(f32)
    )
    mg_ref[...] = grad_gain
    grad_hidden = gy_ref[...].astype(f32) + grad_from_two
    gh_ref[...] = grad_hidden
    grad_low = grad_hidden.astype(bf16)
    ghl_ref[...] = grad_low
    weights_in.wait()
    grad_att = dot_nt(grad_low, ow_ref[...]).astype(bf16)
    cos = cos_ref[...]
    sin = sin_ref[...]
    for seq in range(reps):
        rows = slice(seq * tokens, (seq + 1) * tokens)
        q_all = q_ref[rows, :]
        grad_all = grad_att[rows, :]
        for g in range(KV_HEADS):
            q = head_rows(q_all, g)
            go = head_rows(grad_all, g)
            key_blocks = [key_rows(kv, seq, reps, tokens, g) for kv in kv_refs]
            scores = [
                masked_scores(q, k, mask_ref[p], tokens) for p, k in enumerate(key_blocks)
            ]
            top = functools.reduce(
                jnp.maximum, [jnp.max(s, axis=-1, keepdims=True) for s in scores]
            )
            weights = [jnp.exp(s - top) for s in scores]
            total = functools.reduce(
                jnp.add, [jnp.sum(w, axis=-1, keepdims=True) for w in weights]
            )
            scale = 1.0 / total
            probs = [w * scale for w in weights]
            grad_probs = [
                dot_nt(go, key_rows(kv, seq, reps, tokens, KV_HEADS + g)) for kv in kv_refs
            ]
            delta = functools.reduce(
                jnp.add,
                [jnp.sum(p * d, axis=-1, keepdims=True) for p, d in zip(probs, grad_probs)],
            )
            dq = jnp.zeros((GROUP * tokens, HEAD_DIM), f32)
            for p in range(pieces):
                grad_z = (probs[p] * (grad_probs[p] - delta) * SCALE).astype(bf16)
                dq = dq + dot_nn(grad_z, key_blocks[p])
                dk = dot_tn(grad_z, q).astype(bf16)
                dv = dot_tn(probs[p].astype(bf16), go).astype(bf16)
                stride = reps * tokens
                for a in range(dk.shape[0] // tokens):
                    here = slice(a * stride + seq * tokens, a * stride + (seq + 1) * tokens)
                    part = slice(a * tokens, (a + 1) * tokens)
                    dkv_refs[p][here, g * HEAD_DIM : (g + 1) * HEAD_DIM] = dk[part]
                    v_at = (KV_HEADS + g) * HEAD_DIM
                    dkv_refs[p][here, v_at : v_at + HEAD_DIM] = dv[part]
            for j, block in enumerate(head_columns(dq, tokens)):
                head = g * GROUP + j
                dq_ref[rows, head * HEAD_DIM : (head + 1) * HEAD_DIM] = turn(
                    block, cos, -sin
                ).astype(bf16)


def attend_back(flag, gy, gain, ow, mask, cos, sin, terms, kept, reps):
    tokens, width = gy.shape
    pieces = len(kept) - 2
    versions = len(kept[0])
    arrays = [far(array) for item in kept for array in item]
    piece = kept[2][0]
    keys = pieces * piece.shape[0]
    return call(
        functools.partial(attend_back_kernel, pieces, len(terms), reps, versions),
        (
            jax.ShapeDtypeStruct((tokens, width), f32),
            jax.ShapeDtypeStruct((tokens, width), bf16),
            jax.ShapeDtypeStruct((tokens, QCOLS), bf16),
            jax.ShapeDtypeStruct((1, width), f32),
            *(jax.ShapeDtypeStruct(piece.shape, bf16) for _ in range(pieces)),
        ),
        (flag, gy, gain, far(ow), mask, cos, sin, *terms, *arrays),
        2 * tokens * QCOLS * width + 30 * tokens * QCOLS * keys // reps,
        8 * keys * KCOLS + 20 * tokens * width,
        "attend_back",
        limit=20 + 24 * keys // (reps * 4096),
        in_specs=[SMEM, VMEM, VMEM, ANY] + [VMEM] * (3 + len(terms)) + [ANY] * len(arrays),
        out_specs=(VMEM,) * (4 + pieces),
        scratch_shapes=[
            pltpu.VMEM((tokens, width), f32),
            pltpu.VMEM((tokens, QCOLS), bf16),
            pltpu.VMEM((pieces, *piece.shape), bf16),
            pltpu.SemaphoreType.DMA((2 + pieces,)),
            pltpu.VMEM(ow.shape, bf16),
            pltpu.SemaphoreType.DMA(()),
        ],
    )


def project_back_kernel(terms, reps, versions, *refs):
    (fixed, t_refs, x_refs, outs, scratch), _ = taken(refs, (7, terms, versions, 5, 2))
    flag_ref, dq_ref, gh_ref, gain_ref, w_hbm, cos_ref, sin_ref = fixed
    w_ref, sem = scratch
    copies = column_copies(w_hbm, w_ref, sem)
    gin_ref, gp_ref, n_ref, b_ref, ag_ref = outs
    dkv = sum_refs(t_refs)
    cos = repeat_rows(cos_ref[...], reps)
    sin = repeat_rows(sin_ref[...], reps)
    parts = [
        turn(dkv[:, j * HEAD_DIM : (j + 1) * HEAD_DIM], cos, -sin) for j in range(KV_HEADS)
    ]
    parts.append(dkv[:, KCOLS:])
    gp_ref[:, :QCOLS] = dq_ref[...]
    gp_ref[:, QCOLS:] = jnp.concatenate(parts, axis=1).astype(bf16)
    grad_projected = gp_ref[...]
    b_ref[...] = jnp.sum(grad_projected.astype(f32), axis=0, keepdims=True)
    x = choose(flag_ref, x_refs).astype(f32)
    gain = gain_ref[...].astype(f32)
    n_ref[...] = (x * inverse_rms(x) * gain).astype(bf16)
    grad_normed = jnp.zeros(x.shape, f32)
    tile = 2 * KCOLS
    for k, copy in enumerate(copies):
        here = slice(k * tile, (k + 1) * tile)
        copy.wait()
        grad_normed = grad_normed + dot_nt(grad_projected[:, here], w_ref[:, here])
    grad_source, grad_gain = norm_backward(grad_normed, x, gain)
    ag_ref[...] = grad_gain
    gin_ref[...] = (gh_ref[...] + grad_source).astype(bf16)


def project_back(flag, dq, xs, gh, gain, w, cos, sin, terms, reps):
    tokens, width = gh.shape
    columns = w.shape[1]
    return call(
        functools.partial(project_back_kernel, len(terms), reps, len(xs)),
        (
            jax.ShapeDtypeStruct((tokens, width), bf16),
            jax.ShapeDtypeStruct((tokens, columns), bf16),
            jax.ShapeDtypeStruct((tokens, width), bf16),
            jax.ShapeDtypeStruct((1, columns), f32),
            jax.ShapeDtypeStruct((1, width), f32),
        ),
        (flag, dq, gh, gain, far(w), cos, sin, *terms, *xs),
        2 * tokens * width * columns,
        2 * width * columns,
        "project_back",
        limit=20,
        in_specs=[SMEM] + [VMEM] * 3 + [ANY] + [VMEM] * (2 + len(terms) + len(xs)),
        out_specs=(VMEM,) * 5,
        scratch_shapes=[
            pltpu.VMEM((width, columns), bf16),
            pltpu.SemaphoreType.DMA((columns // (2 * KCOLS),)),
        ],
    )


def attention_grads_kernel(steps, versions, parts, *refs):
    (flags, sources, outs, scratch), _ = taken(refs, (1, 3 * steps + sum(versions), parts, 5))
    at_ref = flags[0]
    n_ref, p_ref, a_ref, h_ref, sem = scratch
    size = n_ref.shape[0] // steps
    copies = []
    groups = []
    targets = []
    for k, target in enumerate((n_ref, p_ref, h_ref)):
        for t in range(steps):
            groups.append((sources[k * steps + t],))
            targets.append(target.at[pl.ds(t * size, size)])
    at = 3 * steps
    for t in range(steps):
        groups.append(sources[at : at + versions[t]])
        targets.append(a_ref.at[pl.ds(t * size, size)])
        at += versions[t]
    copies = bring(at_ref, groups, targets, sem)
    for copy in copies:
        copy.wait()
    columns = p_ref.shape[1]
    rows = outs[0].shape[0]
    for r, out in enumerate(outs):
        here = pl.ds(pl.multiple_of(at_ref[1 + r] * rows, HEAD_DIM), rows)
        out[:, :columns] = dot_tn(n_ref[:, here], p_ref[...]).astype(bf16)
        out[:, columns:] = dot_tn(a_ref[:, here], h_ref[...]).astype(bf16)


def attention_grads(marks, normed, projected, grad_hidden, attended, parts):
    steps = len(normed)
    tokens, width = normed[0].shape
    columns = projected[0].shape[1]
    rows = width // parts
    versions = [len(a) for a in attended]
    arrays = [*normed, *projected, *grad_hidden, *(a for item in attended for a in item)]
    total = steps * tokens
    return call(
        functools.partial(attention_grads_kernel, steps, versions, parts),
        (jax.ShapeDtypeStruct((rows, columns + width), bf16),) * parts,
        (marks, *arrays),
        2 * total * width * (columns + width),
        2 * total * (2 * width + columns) + 2 * width * (width + columns),
        "attention_grads",
        limit=40,
        in_specs=[SMEM] + [ANY] * len(arrays),
        out_specs=(VMEM,) * parts,
        scratch_shapes=[
            pltpu.VMEM((total, width), bf16),
            pltpu.VMEM((total, columns), bf16),
            pltpu.VMEM((total, width), bf16),
            pltpu.VMEM((total, width), bf16),
            pltpu.SemaphoreType.DMA((4 * steps,)),
        ],
    )


def assemble_kernel(pieces, *refs):
    at_ref = refs[0]
    piece_refs = refs[1 : 1 + pieces]
    left_ref, right_ref = refs[-2:]
    columns = left_ref.shape[1]
    rows = piece_refs[0].shape[0]
    for a, piece in enumerate(piece_refs):
        here = pl.ds(pl.multiple_of(at_ref[a] * rows, 8), rows)
        left_ref[here, :] = piece[:, :columns].astype(f32)
        right_ref[here, :] = piece[:, columns:].astype(f32)


def assemble(places, pieces, columns, after):
    rows, total = pieces[0].shape
    count = len(pieces)
    return call(
        functools.partial(assemble_kernel, count),
        (
            jax.ShapeDtypeStruct((rows * count, columns), f32),
            jax.ShapeDtypeStruct((rows * count, total - columns), f32),
        ),
        (places, *pieces, *after),
        0,
        6 * rows * count * total,
        "assemble",
        limit=24,
        in_specs=[SMEM] + [VMEM] * count + [ANY] * len(after),
        out_specs=(VMEM, VMEM),
    )


def unit_tile(units, most):
    return max(t for t in range(16, most + 1, 16) if units % t == 0)


def weight_grad_kernel(aliased, adds, *refs):
    n_ref, g_ref, gate_ref, up_ref, down_ref = refs[:5]
    olds = refs[5 : 5 + aliased]
    news = refs[-4:-1]
    refs[-1][...] = jnp.zeros_like(refs[-1])

    @pl.when(pl.program_id(1) == 0)
    def _():
        for k, new in enumerate(news):
            new[...] = olds[k][...] if adds else jnp.zeros_like(new)

    rows = n_ref[...]
    grads = g_ref[...]
    gate_pre = dot_nt(gate_ref[...], rows)
    up_pre = dot_nt(up_ref[...], rows)
    grad_act = dot_nt(down_ref[...], grads)
    silu, grad_gate, grad_up = swiglu_backward(gate_pre, up_pre, grad_act)
    activated = (silu * up_pre).astype(bf16)
    news[0][...] += dot_nn(grad_gate, rows)
    news[1][...] += dot_nn(grad_up, rows)
    news[2][...] += dot_nn(activated, grads)


def weight_grads(n_all, g_all, gate, up, down, outs, adds, first, count, after):
    units, width = gate.shape
    tokens = n_all.shape[0]
    tile = unit_tile(units, 320)
    chunk = math.gcd(tokens, 1024)
    shape = jax.ShapeDtypeStruct((units, width), f32)
    part = pl.BlockSpec((tile, width), lambda i, j: (i + first, 0))
    rows = pl.BlockSpec((chunk, width), lambda i, j: (j, 0))
    *outs, zeros = call(
        functools.partial(weight_grad_kernel, len(outs), adds),
        (*(shape,) * 3, jax.ShapeDtypeStruct((8, 128), f32)),
        (n_all, g_all, gate, up, down, *outs, *after),
        12 * tokens * width * tile * count,
        18 * width * tile * count,
        "weight_grads",
        limit=60,
        grid=(count, tokens // chunk),
        in_specs=[rows] * 2
        + [part] * 3
        + [part if adds else ANY] * len(outs)
        + [ANY] * len(after),
        out_specs=((*(part,) * 3, pl.BlockSpec((8, 128), lambda i, j: (0, 0)))),
        input_output_aliases={5 + k: k for k in range(len(outs))},
    )
    return outs, zeros


def body(
    inputs,
    cotangent,
    attn_gain,
    qkv_weight,
    qkv_bias,
    out_weight,
    mlp_gain,
    gate_weight,
    up_weight,
    down_weight,
):
    first = lax.axis_index("section") == 0
    micro, rows_here, _, width = inputs.shape
    fsdp = lax.axis_size("fsdp")
    ctx = lax.axis_size("ctx")
    fsdp_at = lax.axis_index("fsdp")
    ctx_at = lax.axis_index("ctx")
    tokens = 2 * rows_here
    reps = MICROS
    chunks = micro // reps
    steps = chunks + LAG
    span_rows = rows_here * fsdp
    half_rows = span_rows * ctx

    def places_of(c, f):
        index = (c * fsdp + f) * rows_here + jnp.arange(rows_here, dtype=jnp.int32)
        return storage_place(index, span_rows, half_rows).reshape(tokens)

    own = places_of(ctx_at, fsdp_at)
    key_places = jnp.stack(
        [
            jnp.concatenate([places_of(ctx_at ^ a, fsdp_at ^ r) for a in range(ctx)])
            for r in relative_order(fsdp)
        ]
    )
    mask = jnp.where(key_places[:, None, :] <= own[None, :, None], 0.0, NEGATIVE).astype(f32)
    half = HEAD_DIM // 2
    frequency = ROPE_BASE ** (-(jnp.arange(half, dtype=f32) * 2.0) / HEAD_DIM)
    angles = own.astype(f32)[:, None] * frequency
    cos = jnp.concatenate([jnp.cos(angles)] * 2, axis=1)
    sin = jnp.concatenate([-jnp.sin(angles), jnp.sin(angles)], axis=1)

    def gathered(shard):
        return lax.all_gather(shard, "fsdp", axis=0, tiled=True)

    qkv_full = gathered(qkv_weight[0])
    attn_full = gathered(attn_gain[0])[None]
    bias_full = gathered(qkv_bias[0])[None]
    mlp_full = gathered(mlp_gain[0])[None]
    out_full = gathered(out_weight[0])
    gate, up, down = gate_weight[0], up_weight[0], down_weight[0]

    def chunked(array):
        return array.reshape(chunks, reps * tokens, width)

    in_chunks = chunked(inputs)
    cot_chunks = chunked(cotangent)

    gate_held, up_held, down_held = hold(gate, up, down)
    flag = first.astype(jnp.int32).reshape(1)

    def pick(early, late):
        return jnp.where(first, early, late)

    def versions(u, early, late):
        if u < LAG:
            return (late[u + LAG],)
        if u < chunks:
            return (early[u - LAG], late[u + LAG])
        return (early[u - LAG],)

    gys = [jnp.where(first, jnp.zeros_like(cot), cot) for cot in cot_chunks[:LAG]]
    early_pieces = [gather_pieces(gy, "fsdp") for gy in gys]

    outputs, moved, xs, kept, attended, n2_pieces = [], [], [], [], [], []

    def finish(t, after=()):
        parts = mlp(n2_pieces[t], gate_held, up_held, down_held, after)
        hidden = kept[t][0]
        outputs.append(add_low([hidden] + reduce_pieces(list(parts), "fsdp")))
        if t < chunks:
            moved.append(passed_along(outputs[t], "section", 1))

    for t in range(steps):
        if t < LAG:
            x = (in_chunks[t],)
        elif t < chunks:
            x = (in_chunks[t], moved[t - LAG])
        else:
            x = (moved[t - LAG],)
        xs.append(x)
        after = [p for pieces in early_pieces for p in pieces[1:]] if t == 0 else []
        q, kv = project(flag, x, attn_full, qkv_full, bias_full, cos, sin, reps, after)
        kv_ctx = jnp.concatenate([kv] + [exchange(kv, "ctx", a) for a in range(1, ctx)], axis=0)
        kv_pieces = gather_pieces(kv_ctx, "fsdp")
        att, hidden, n2 = attend(flag, q, x, mask, out_full, mlp_full, kv_pieces, reps)
        attended.append(att)
        n2_pieces.append(gather_pieces(n2, "fsdp"))
        kept.append((hidden, q, *kv_pieces))
        if t < chunks:
            finish(t)

    batches = [b for b in (range(0, chunks // 2), range(chunks // 2, chunks)) if len(b)]

    def all_tokens(early, late, batch):
        own_rows = jnp.concatenate([pick(early[m], late[m]) for m in batch], axis=0)
        return lax.all_gather(own_rows, ("ctx", "fsdp"), axis=0, tiled=True)

    n2_own = [pieces[0] for pieces in n2_pieces]
    n2_all = [all_tokens(n2_own, n2_own[LAG:], batch) for batch in batches]

    grads_in, grads_moved, smalls, factors = [], [], [], []
    for u in range(steps):
        if u < LAG:
            gy, g_pieces = gys[u], early_pieces[u]
        else:
            gy = grads_moved[u - LAG]
            gy = pick(gy, cot_chunks[u]) if u < chunks else gy
            gys.append(gy)
            g_pieces = gather_pieces(gy, "fsdp")
        after = [outputs[u + LAG]] if u + LAG < chunks else []
        n2_now = list(zip(*versions(u, n2_pieces, n2_pieces)))
        parts = mlp_back(flag, n2_now, g_pieces, gate_held, up_held, down_held, after)
        terms = reduce_pieces(list(parts), "fsdp")
        kept_now = list(zip(*versions(u, kept, kept)))
        gh, gh_low, dq, grad_mlp_gain, *dkv = attend_back(
            flag, gy, mlp_full, out_full, mask, cos, sin, terms, kept_now, reps
        )
        dkv_ctx = add_low(reduce_pieces(dkv, "fsdp"))
        size = reps * tokens
        dkv_terms = [
            dkv_ctx[a * size : (a + 1) * size]
            if a == 0
            else exchange(dkv_ctx[a * size : (a + 1) * size], "ctx", a)
            for a in range(ctx)
        ]
        x_early = [x[0] for x in xs]
        x_late = [x[-1] for x in xs]
        x_now = versions(u, x_early, x_late)
        g_in, g_proj, normed, grad_bias, grad_attn_gain = project_back(
            flag, dq, x_now, gh, attn_full, qkv_full, cos, sin, dkv_terms, reps
        )
        grads_in.append(g_in)
        if u < chunks:
            grads_moved.append(passed_along(g_in, "section", -1))
        smalls.append(jnp.concatenate([grad_attn_gain, grad_bias, grad_mlp_gain], axis=1))
        factors.append((normed, g_proj, gh_low, versions(u, attended, attended)))
        if u >= LAG and len(outputs) < steps:
            finish(len(outputs), [g_in])

    g_all = [all_tokens(gys[LAG:], gys, batch) for batch in batches]
    tiles = gate.shape[0] // unit_tile(gate.shape[0], 320)
    cuts = [0, 4 * tiles // 7, tiles], [0, tiles // 7, 5 * tiles // 7, tiles]
    plan = [
        (b, i, j - i)
        for b in range(len(batches))
        for i, j in zip(cuts[b], cuts[b][1:])
        if j > i
    ]
    mlp_grads = []

    def some_weight_grads(after):
        nonlocal mlp_grads
        if not plan:
            return None
        b, start, count = plan.pop(0)
        mlp_grads, zeros = weight_grads(
            n2_all[b], g_all[b], gate, up, down, mlp_grads, b > 0, start, count, after
        )
        return zeros

    lead = QCOLS + KCOLS
    columns = QCOLS + 2 * KCOLS
    marks = jnp.stack(
        [flag[0]] + [(fsdp_at ^ r).astype(jnp.int32) for r in relative_order(fsdp)]
    )
    normed, projected, grad_hidden, att_now = zip(*factors)
    small = functools.reduce(jnp.add, smalls).reshape(-1, HEAD_DIM)
    rows = width // fsdp
    if rows % HEAD_DIM == 0:
        summed = attention_grads(marks, normed, projected, grad_hidden, att_now, fsdp)
    else:
        start = jnp.stack([flag[0], jnp.int32(0)])
        (large,) = attention_grads(start, normed, projected, grad_hidden, att_now, 1)
        summed = [
            lax.dynamic_slice_in_dim(large, (fsdp_at ^ r) * rows, rows)
            for r in relative_order(fsdp)
        ]
    for bit in reversed(bits_of(fsdp)):
        count = len(summed) // 2
        moves = [exchange(p, "fsdp", bit) for p in summed[count:]]
        zero = 0.0
        if count == 1:
            zero = some_weight_grads([*summed[:1], *outputs[chunks:]])[0, 0]
        summed = [
            (p.astype(f32) + m.astype(f32) + zero).astype(bf16) for p, m in zip(summed, moves)
        ]
        small = small + exchange(small, "fsdp", bit)
    rows = width // fsdp // ctx
    terms = [
        lax.dynamic_slice_in_dim(summed[0], (ctx_at ^ a) * rows, rows) for a in range(ctx)
    ]
    moves = [exchange(terms[a], "ctx", a) for a in range(1, ctx)]
    for bit in bits_of(ctx):
        small = small + exchange(small, "ctx", bit)
    zeros = some_weight_grads(terms[:1])
    zeros = some_weight_grads([]) if plan else zeros
    block = functools.reduce(jnp.add, [t.astype(f32) for t in (terms[0], *moves)])
    block = (block + zeros[0, 0]).astype(bf16)
    pieces = [block] + [exchange(block, "ctx", a) for a in range(1, ctx)]
    zeros = some_weight_grads([block])
    places = jnp.stack([(ctx_at ^ a).astype(jnp.int32) for a in range(ctx)])
    grad_qkv, grad_out = assemble(places, pieces, columns, [] if zeros is None else [zeros])
    while plan:
        some_weight_grads([])
    grad_gate, grad_up, grad_down = mlp_grads

    small = small.reshape(-1)

    def cut(start, length):
        part = length // fsdp
        return lax.dynamic_slice(small, (start + fsdp_at * part,), (part,))

    grad_attn_gain = cut(0, width)
    grad_bias_lead = cut(width, lead)
    grad_bias_value = cut(width + lead, columns - lead)
    grad_mlp_gain = cut(width + columns, width)

    def restore(parts):
        return jnp.stack(parts).reshape(inputs.shape)

    layer_outputs = restore([pick(outputs[m], outputs[m + LAG]) for m in range(chunks)])
    input_grads = restore([pick(grads_in[m + LAG], grads_in[m]) for m in range(chunks)])
    return (
        layer_outputs[None],
        input_grads[None],
        grad_attn_gain[None],
        grad_qkv[None],
        grad_bias_lead[None],
        grad_bias_value[None],
        grad_out[None],
        grad_mlp_gain[None],
        grad_gate[None],
        grad_up[None],
        grad_down[None],
    )


def solution(mesh):
    rows = P(None, ("ctx", "fsdp"), None, None)
    vector = P("section", "fsdp")
    matrix = P("section", "fsdp", None)
    stacked = P("section", None, ("ctx", "fsdp"), None, None)
    in_specs = (rows, rows, vector, matrix, vector, matrix, vector, matrix, matrix, matrix)
    out_specs = (
        stacked,
        stacked,
        vector,
        matrix,
        vector,
        vector,
        matrix,
        vector,
        matrix,
        matrix,
        matrix,
    )
    return jax.shard_map(body, mesh=mesh, in_specs=in_specs, out_specs=out_specs, check_vma=False)
```

```python
import functools
import math

import jax
import jax.numpy as jnp
from jax import lax
from jax.experimental import pallas as pl
from jax.experimental.pallas import tpu as pltpu
from jax.sharding import PartitionSpec as P

HEADS = 12
KV_HEADS = 2
HEAD_DIM = 128
GROUP = HEADS // KV_HEADS
EPS = 1e-06
ROPE_BASE = 1000000.0
NEGATIVE = -1e30
QCOLS = HEADS * HEAD_DIM
KCOLS = KV_HEADS * HEAD_DIM
SCALE = HEAD_DIM ** (-0.5)

MICROS = 2
LAG = 1
FORWARD = "KJQAMRY"
SEQUENCE = (
    "K0 J0 Q0 A0 H M0 R0 Y0 K1 Q1 J1 A1 H M1 R1 "
    "B0 Y1 S0 K2 T0 D0 J2 Q2 E0 P0 A2 G1 H "
    "B1 S1 T1 D1 E1 P1 G2 H B2 M2 S2 T2 D2 E2 P2 "
)
ROWS = 16
UNITS = 512

f32 = jnp.float32
bf16 = jnp.bfloat16
MIB = 1 << 20


def dot_nn(a, b):
    return lax.dot_general(a, b, (((1,), (0,)), ((), ())), preferred_element_type=f32)


def dot_nt(a, b):
    return lax.dot_general(a, b, (((1,), (1,)), ((), ())), preferred_element_type=f32)


def dot_tn(a, b):
    return lax.dot_general(a, b, (((0,), (0,)), ((), ())), preferred_element_type=f32)


def inverse_rms(values):
    return lax.rsqrt(jnp.mean(values * values, axis=-1, keepdims=True) + EPS)


def norm_backward(grad_normed, values, gain):
    inverse = inverse_rms(values)
    scaled = grad_normed * gain
    grad_values = inverse * scaled - values * (
        inverse**3 * jnp.mean(scaled * values, axis=-1, keepdims=True)
    )
    grad_gain = jnp.sum(grad_normed * values * inverse, axis=0, keepdims=True)
    return grad_values, grad_gain


def exchange(block, axis, mask):
    size = lax.axis_size(axis)
    return lax.ppermute(block, axis, [(i, i ^ mask) for i in range(size)])


def passed_along(block, axis, distance):
    devices = range(lax.axis_size(axis))
    route = [(i - distance, i) for i in devices if i - distance in devices]
    return lax.ppermute(block, axis, route)


def bits_of(size):
    return [1 << b for b in reversed(range(size.bit_length() - 1))]


def relative_order(size):
    order = [0]
    for bit in bits_of(size):
        order = order + [r ^ bit for r in order]
    return order


def gather_pieces(block, axis):
    pieces = [block]
    for bit in bits_of(lax.axis_size(axis)):
        pieces = pieces + [exchange(p, axis, bit) for p in pieces]
    return pieces


def reduction(near, far_half, axis, total):
    terms = [near]
    sent = far_half
    extent = near.shape[0]
    bits = bits_of(lax.axis_size(axis))[::-1]
    for k, bit in enumerate(bits):
        if k > 0:
            extent //= 2
            sent = total(terms, extent)
        terms.append(exchange(sent, axis, bit))
        yield
    return terms


ORDER = []


def call(
    kernel, out_shape, args, flops, moved, name, in_specs, limit=24, after=(), ordered=True, **kwargs
):
    waits = [*after, *(ORDER if ordered else ())]

    def body(*refs):
        kernel(*refs[len(waits) :])

    result = pl.pallas_call(
        body,
        out_shape=out_shape,
        in_specs=[*[ANY] * len(waits), *in_specs],
        compiler_params=pltpu.CompilerParams(vmem_limit_bytes=limit * MIB),
        cost_estimate=pl.CostEstimate(flops=flops, bytes_accessed=moved, transcendentals=0),
        name=name,
        **kwargs,
    )(*waits, *args)
    if ordered:
        ORDER[:] = [result[0] if isinstance(result, (tuple, list)) else result]
    return result


ANY = pl.BlockSpec(memory_space=pl.ANY)
VMEM = pl.BlockSpec(memory_space=pltpu.VMEM)
SMEM = pl.BlockSpec(memory_space=pltpu.SMEM)


def hold_kernel(count, *refs):
    copies = [
        pltpu.make_async_copy(refs[k], refs[count + k], refs[-1].at[k]) for k in range(count)
    ]
    for copy in copies:
        copy.start()
    wait_all(copies)


def hold(*arrays):
    return call(
        functools.partial(hold_kernel, len(arrays)),
        tuple(pltpu.VMEM(a.shape, a.dtype) for a in arrays),
        [far(a) for a in arrays],
        0,
        2 * sum(a.size for a in arrays),
        "hold",
        limit=4,
        in_specs=[ANY] * len(arrays),
        out_specs=tuple(VMEM for _ in arrays),
        scratch_shapes=[pltpu.SemaphoreType.DMA((len(arrays),))],
    )


def held(array):
    return pltpu.with_memory_space_constraint(array, pltpu.VMEM)


def far(array):
    return pltpu.with_memory_space_constraint(array, pltpu.HBM)


def bring(marks_ref, sources, targets, sem):
    copies = []
    for k, (source, target) in enumerate(zip(sources, targets)):
        if len(source) == 1:
            copy = pltpu.make_async_copy(source[0], target, sem.at[k])
            copy.start()
        else:
            for is_first, ref in zip((1, 0), source):
                copy = pltpu.make_async_copy(ref, target, sem.at[k])
                pl.when(marks_ref[0] == is_first)(copy.start)
        copies.append(copy)
    return copies


def taken(refs, counts):
    groups = []
    for count in counts:
        groups.append(refs[:count])
        refs = refs[count:]
    return groups, refs


def turn(value, cos, sin):
    return value * cos + pltpu.roll(value, HEAD_DIM // 2, 1) * sin


def repeat_rows(table, count):
    return table if count == 1 else jnp.concatenate([table] * count, axis=0)


def choose(marks_ref, refs):
    if len(refs) == 1:
        return refs[0][...]
    return jnp.where(marks_ref[0] == 1, refs[0][...], refs[1][...])


def weight_copies(starts_ref, pieces, target, sem, tile=None):
    columns = target.shape[1]
    tile = tile or columns
    tiles = []
    for k in range(columns // tile):
        copies = []
        for r, piece in enumerate(pieces):
            at = pl.multiple_of(starts_ref[r] * ROWS, ROWS)
            there = target.at[pl.ds(at, piece.shape[0]), pl.ds(k * tile, tile)]
            copy = pltpu.make_async_copy(piece.at[:, pl.ds(k * tile, tile)], there, sem.at[k, r])
            copy.start()
            copies.append(copy)
        tiles.append(copies)
    return tiles


def wait_all(copies):
    for copy in copies:
        copy.wait()


def project_kernel(reps, versions, pieces, turned_heads, tile, *refs):
    (fixed, w_refs, x_refs), rest = taken(refs, (6, pieces, versions))
    marks_ref, starts_ref, gain_ref, b_ref, cos_ref, sin_ref = fixed
    out_ref, n_ref, w_ref, sem = rest[-4:]
    tiles = weight_copies(starts_ref, w_refs, w_ref, sem, tile)
    x = choose(marks_ref, x_refs).astype(f32)
    n_ref[...] = (x * inverse_rms(x) * gain_ref[...].astype(f32)).astype(bf16)
    cos = repeat_rows(cos_ref[...], reps)
    sin = repeat_rows(sin_ref[...], reps)
    for k, copies in enumerate(tiles):
        here = slice(k * tile, (k + 1) * tile)
        wait_all(copies)
        projected = dot_nn(n_ref[...], w_ref[:, here]) + b_ref[:, here].astype(f32)
        turned = []
        for j in range(tile // HEAD_DIM):
            part = projected[:, j * HEAD_DIM : (j + 1) * HEAD_DIM]
            head = k * tile // HEAD_DIM + j
            turned.append(turn(part, cos, sin) if head < turned_heads else part)
        out_ref[:, here] = jnp.concatenate(turned, axis=1).astype(bf16)


def project(marks, xs, gain, weight, b, cos, sin, reps, turned_heads, after=()):
    w_pieces, starts = weight
    tokens, width = xs[0].shape
    columns = w_pieces[0].shape[1]
    tile = 2 * KCOLS
    count = len(w_pieces)
    return call(
        functools.partial(project_kernel, reps, len(xs), count, turned_heads, tile),
        jax.ShapeDtypeStruct((tokens, columns), bf16),
        (marks, starts, gain, b, cos, sin, *(far(w) for w in w_pieces), *xs),
        2 * tokens * width * columns,
        2 * width * columns,
        "project",
        limit=16,
        in_specs=[SMEM] * 2 + [VMEM] * 4 + [ANY] * count + [VMEM] * len(xs),
        after=after,
        out_specs=VMEM,
        scratch_shapes=[
            pltpu.VMEM((tokens, width), bf16),
            pltpu.VMEM((width, columns), bf16),
            pltpu.SemaphoreType.DMA((columns // tile, count)),
        ],
    )


def head_rows(block, g):
    return jnp.concatenate(
        [
            block[:, (g * GROUP + j) * HEAD_DIM : (g * GROUP + j + 1) * HEAD_DIM]
            for j in range(GROUP)
        ],
        axis=0,
    )


def head_columns(rows, tokens):
    return [rows[j * tokens : (j + 1) * tokens] for j in range(GROUP)]


def key_rows(ref, seq, reps, tokens, column):
    columns = slice(column * HEAD_DIM, (column + 1) * HEAD_DIM)
    if reps == 1:
        return ref[:, columns]
    stride = reps * tokens
    return jnp.concatenate(
        [
            ref[a * stride + seq * tokens : a * stride + (seq + 1) * tokens, columns]
            for a in range(ref.shape[0] // stride)
        ],
        axis=0,
    )


def masked_scores(q, key_block, mask, tokens):
    scores = dot_nt(q, key_block) * SCALE
    keys = scores.shape[1]
    return (scores.reshape(GROUP, tokens, keys) + mask[None]).reshape(GROUP * tokens, keys)


def attend_kernel(pieces, weights, reps, versions, *refs):
    (fixed, ow_refs, kv_refs, x_refs), rest = taken(refs, (5, weights, pieces, versions))
    marks_ref, starts_ref, q_ref, mask_ref, gain_ref = fixed
    att_ref, hid_ref, n2_ref, ow_ref, sem = rest[-5:]
    (weights_in,) = weight_copies(starts_ref, ow_refs, ow_ref, sem)
    tokens = q_ref.shape[0] // reps
    for seq in range(reps):
        rows = slice(seq * tokens, (seq + 1) * tokens)
        q_all = q_ref[rows, :]
        for g in range(KV_HEADS):
            q = head_rows(q_all, g)
            scores = [
                masked_scores(q, key_rows(kv, seq, reps, tokens, g), mask_ref[p], tokens)
                for p, kv in enumerate(kv_refs)
            ]
            top = functools.reduce(
                jnp.maximum, [jnp.max(s, axis=-1, keepdims=True) for s in scores]
            )
            total = jnp.zeros_like(top)
            acc = jnp.zeros((GROUP * tokens, HEAD_DIM), f32)
            for s, kv in zip(scores, kv_refs):
                weights = jnp.exp(s - top)
                total = total + jnp.sum(weights, axis=-1, keepdims=True)
                acc = acc + dot_nn(
                    weights.astype(bf16), key_rows(kv, seq, reps, tokens, KV_HEADS + g)
                )
            low = (acc / total).astype(bf16)
            for j, block in enumerate(head_columns(low, tokens)):
                head = g * GROUP + j
                att_ref[rows, head * HEAD_DIM : (head + 1) * HEAD_DIM] = block
    wait_all(weights_in)
    hidden = choose(marks_ref, x_refs).astype(f32) + dot_nn(att_ref[...], ow_ref[...])
    hid_ref[...] = hidden
    n2_ref[...] = (hidden * inverse_rms(hidden) * gain_ref[...].astype(f32)).astype(bf16)


def attend(marks, q, xs, mask, weight, gain, kv_pieces, reps, after=()):
    ow_pieces, starts = weight
    tokens, width = xs[0].shape
    keys = sum(p.shape[0] for p in kv_pieces)
    return call(
        functools.partial(attend_kernel, len(kv_pieces), len(ow_pieces), reps, len(xs)),
        (
            jax.ShapeDtypeStruct((tokens, QCOLS), bf16),
            jax.ShapeDtypeStruct((tokens, width), f32),
            jax.ShapeDtypeStruct((tokens, width), bf16),
        ),
        (marks, starts, q, mask, gain, *(far(w) for w in ow_pieces), *kv_pieces, *xs),
        2 * tokens * QCOLS * width + 12 * tokens * QCOLS * keys // reps,
        4 * keys * KCOLS + 12 * tokens * width,
        "attend",
        limit=16 + 24 * keys // (reps * 4096),
        in_specs=[SMEM] * 2
        + [VMEM] * 3
        + [ANY] * len(ow_pieces)
        + [VMEM] * (len(kv_pieces) + len(xs)),
        after=after,
        out_specs=(VMEM,) * 3,
        scratch_shapes=[
            pltpu.VMEM((QCOLS, width), bf16),
            pltpu.SemaphoreType.DMA((1, len(ow_pieces))),
        ],
    )


def fill(scratch, refs):
    size = refs[0].shape[0]
    for p, ref in enumerate(refs):
        scratch[p * size : (p + 1) * size, :] = ref[...]


def spread(out_refs, acc_ref):
    fill_from = 0
    for ref in out_refs:
        ref[...] = acc_ref[fill_from : fill_from + ref.shape[0], :].astype(bf16)
        fill_from += ref.shape[0]


def unit_spans(units):
    return [slice(at, min(at + UNITS, units)) for at in range(0, units, UNITS)]


def mlp_kernel(pieces, *refs):
    n_refs = refs[:pieces]
    gate_ref, up_ref, down_ref = refs[pieces : pieces + 3]
    out_refs = refs[-4:-2]
    cat_ref, acc_ref = refs[-2:]
    fill(cat_ref, n_refs)
    for k, here in enumerate(unit_spans(gate_ref.shape[0])):
        rows = cat_ref[...]
        gate_pre = dot_nt(rows, gate_ref[here, :])
        up_pre = dot_nt(rows, up_ref[here, :])
        activated = (jax.nn.sigmoid(gate_pre) * gate_pre * up_pre).astype(bf16)
        term = dot_nn(activated, down_ref[here, :])
        if k == 0:
            acc_ref[...] = term
        else:
            acc_ref[...] += term
    spread(out_refs, acc_ref)


def mlp(n_pieces, gate, up, down, after=()):
    units, width = gate.shape
    tokens = n_pieces[0].shape[0]
    count = len(n_pieces)
    return call(
        functools.partial(mlp_kernel, count),
        (jax.ShapeDtypeStruct((count // 2 * tokens, width), bf16),) * 2,
        (*n_pieces, held(gate), held(up), held(down)),
        6 * count * tokens * width * units,
        4 * count * tokens * width,
        "mlp",
        limit=12 * max(1, count * tokens // 512),
        in_specs=[VMEM] * (count + 3),
        after=after,
        out_specs=(VMEM,) * 2,
        scratch_shapes=[
            pltpu.VMEM((count * tokens, width), bf16),
            pltpu.VMEM((count * tokens, width), f32),
        ],
    )


def swiglu_backward(gate_pre, up_pre, grad_act):
    sigmoid = jax.nn.sigmoid(gate_pre)
    silu = gate_pre * sigmoid
    grad_gate = (grad_act * up_pre * (sigmoid + silu * (1.0 - sigmoid))).astype(bf16)
    grad_up = (grad_act * silu).astype(bf16)
    return silu, grad_gate, grad_up


def mlp_back_kernel(pieces, versions, *refs):
    (flags, weights, n_refs, g_refs), rest = taken(
        refs, (1, 3, pieces * versions, pieces)
    )
    gate_ref, up_ref, down_ref = weights
    out_refs = rest[-6:-4]
    cat_ref, gcat_ref, acc_ref, sem = rest[-4:]
    size = cat_ref.shape[0] // pieces
    spans = [pl.ds(p * size, size) for p in range(pieces)]
    sources = [n_refs[p * versions : (p + 1) * versions] for p in range(pieces)]
    copies = bring(
        flags[0],
        sources + [(g,) for g in g_refs],
        [cat_ref.at[span] for span in spans] + [gcat_ref.at[span] for span in spans],
        sem,
    )
    for copy in copies:
        copy.wait()
    for k, here in enumerate(unit_spans(gate_ref.shape[0])):
        rows = cat_ref[...]
        gate_pre = dot_nt(rows, gate_ref[here, :])
        up_pre = dot_nt(rows, up_ref[here, :])
        grad_act = dot_nt(gcat_ref[...], down_ref[here, :])
        _, grad_gate, grad_up = swiglu_backward(gate_pre, up_pre, grad_act)
        term = dot_nn(grad_gate, gate_ref[here, :]) + dot_nn(grad_up, up_ref[here, :])
        if k == 0:
            acc_ref[...] = term
        else:
            acc_ref[...] += term
    spread(out_refs, acc_ref)


def mlp_back(flag, n_versions, g_pieces, gate, up, down, after):
    units, width = gate.shape
    tokens = g_pieces[0].shape[0]
    count = len(g_pieces)
    versions = len(n_versions[0])
    n_arrays = [far(array) for piece in n_versions for array in piece]
    return call(
        functools.partial(mlp_back_kernel, count, versions),
        (jax.ShapeDtypeStruct((count // 2 * tokens, width), bf16),) * 2,
        (flag, held(gate), held(up), held(down), *n_arrays, *g_pieces),
        10 * count * tokens * width * units,
        6 * count * tokens * width,
        "mlp_back",
        limit=16 * max(1, count * tokens // 512),
        in_specs=[SMEM] + [VMEM] * 3 + [ANY] * (len(n_arrays) + count),
        after=after,
        out_specs=(VMEM,) * 2,
        scratch_shapes=[
            pltpu.VMEM((count * tokens, width), bf16),
            pltpu.VMEM((count * tokens, width), bf16),
            pltpu.VMEM((count * tokens, width), f32),
            pltpu.SemaphoreType.DMA((2 * count,)),
        ],
    )


def sum_refs(refs, rows=None):
    rows = rows or refs[0].shape[0]
    total = refs[0][:rows, :].astype(f32)
    for ref in refs[1:]:
        total = total + ref[:rows, :].astype(f32)
    return total


def attend_back_kernel(pieces, weights, terms, reps, versions, *refs):
    (fixed, ow_refs, t_refs, sources, outs, dkv_refs, scratch), _ = taken(
        refs, (7, weights, terms, (2 + pieces) * versions, 4, 2, 6)
    )
    marks_ref, starts_ref, gy_ref, gain_ref, mask_ref, cos_ref, sin_ref = fixed
    gh_ref, ghl_ref, dq_ref, mg_ref = outs
    hid_ref, q_ref, kv_ref, sem, ow_ref, ow_sem = scratch
    kv_refs = [kv_ref.at[p] for p in range(pieces)]
    *copies, hidden_in = bring(
        marks_ref,
        [sources[k * versions : (k + 1) * versions] for k in (*range(1, 2 + pieces), 0)],
        [q_ref, *kv_refs, hid_ref],
        sem,
    )
    (weights_in,) = weight_copies(starts_ref, ow_refs, ow_ref, ow_sem)
    tokens = q_ref.shape[0] // reps
    wait_all(copies)
    places = [(seq, g) for seq in range(reps) for g in range(KV_HEADS)]
    probs_at = {}
    for seq, g in places:
        q = head_rows(q_ref[seq * tokens : (seq + 1) * tokens, :], g)
        scores = [
            masked_scores(q, key_rows(kv, seq, reps, tokens, g), mask_ref[p], tokens)
            for p, kv in enumerate(kv_refs)
        ]
        top = functools.reduce(jnp.maximum, [jnp.max(s, axis=-1, keepdims=True) for s in scores])
        weights = [jnp.exp(s - top) for s in scores]
        total = functools.reduce(jnp.add, [jnp.sum(w, axis=-1, keepdims=True) for w in weights])
        scale = 1.0 / total
        probs_at[seq, g] = [w * scale for w in weights]
    hidden_in.wait()
    grad_from_two, grad_gain = norm_backward(
        sum_refs(t_refs, hid_ref.shape[0]), hid_ref[...], gain_ref[...].astype(f32)
    )
    mg_ref[...] = grad_gain
    grad_hidden = gy_ref[...].astype(f32) + grad_from_two
    gh_ref[...] = grad_hidden
    grad_low = grad_hidden.astype(bf16)
    ghl_ref[...] = grad_low
    wait_all(weights_in)
    grad_att = dot_nt(grad_low, ow_ref[...]).astype(bf16)
    cos = cos_ref[...]
    sin = sin_ref[...]
    for seq, g in places:
        rows = slice(seq * tokens, (seq + 1) * tokens)
        q = head_rows(q_ref[rows, :], g)
        go = head_rows(grad_att[rows, :], g)
        probs = probs_at[seq, g]
        grad_probs = [
            dot_nt(go, key_rows(kv, seq, reps, tokens, KV_HEADS + g)) for kv in kv_refs
        ]
        delta = functools.reduce(
            jnp.add,
            [jnp.sum(p * d, axis=-1, keepdims=True) for p, d in zip(probs, grad_probs)],
        )
        dq = jnp.zeros((GROUP * tokens, HEAD_DIM), f32)
        for p in range(pieces):
            grad_z = (probs[p] * (grad_probs[p] - delta) * SCALE).astype(bf16)
            dq = dq + dot_nn(grad_z, key_rows(kv_refs[p], seq, reps, tokens, g))
            dk = dot_tn(grad_z, q).astype(bf16)
            dv = dot_tn(probs[p].astype(bf16), go).astype(bf16)
            stride = reps * tokens
            dkv_ref = dkv_refs[p // (pieces // 2)]
            base = p % (pieces // 2) * kv_ref.shape[1] + seq * tokens
            for a in range(dk.shape[0] // tokens):
                here = slice(base + a * stride, base + a * stride + tokens)
                part = slice(a * tokens, (a + 1) * tokens)
                dkv_ref[here, g * HEAD_DIM : (g + 1) * HEAD_DIM] = dk[part]
                v_at = (KV_HEADS + g) * HEAD_DIM
                dkv_ref[here, v_at : v_at + HEAD_DIM] = dv[part]
        for j, block in enumerate(head_columns(dq, tokens)):
            head = g * GROUP + j
            dq_ref[rows, head * HEAD_DIM : (head + 1) * HEAD_DIM] = turn(
                block, cos, -sin
            ).astype(bf16)


def attend_back(marks, gy, gain, weight, mask, cos, sin, terms, kept, reps):
    ow_pieces, starts = weight
    tokens, width = gy.shape
    pieces = len(kept) - 2
    versions = len(kept[0])
    arrays = [far(array) for item in kept for array in item]
    piece = kept[2][0]
    keys = pieces * piece.shape[0]
    return call(
        functools.partial(
            attend_back_kernel, pieces, len(ow_pieces), len(terms), reps, versions
        ),
        (
            jax.ShapeDtypeStruct((tokens, width), f32),
            jax.ShapeDtypeStruct((tokens, width), bf16),
            jax.ShapeDtypeStruct((tokens, QCOLS), bf16),
            jax.ShapeDtypeStruct((1, width), f32),
            *(jax.ShapeDtypeStruct((pieces // 2 * piece.shape[0], piece.shape[1]), bf16),) * 2,
        ),
        (marks, starts, gy, gain, mask, cos, sin, *(far(w) for w in ow_pieces), *terms, *arrays),
        2 * tokens * QCOLS * width + 30 * tokens * QCOLS * keys // reps,
        8 * keys * KCOLS + 20 * tokens * width,
        "attend_back",
        limit=20 + 40 * keys // (reps * 4096),
        in_specs=[SMEM] * 2
        + [VMEM] * 5
        + [ANY] * len(ow_pieces)
        + [VMEM] * len(terms)
        + [ANY] * len(arrays),
        out_specs=(VMEM,) * 6,
        scratch_shapes=[
            pltpu.VMEM((tokens, width), f32),
            pltpu.VMEM((tokens, QCOLS), bf16),
            pltpu.VMEM((pieces, *piece.shape), bf16),
            pltpu.SemaphoreType.DMA((2 + pieces,)),
            pltpu.VMEM((QCOLS, width), bf16),
            pltpu.SemaphoreType.DMA((1, len(ow_pieces))),
        ],
    )


def project_back_kernel(terms, reps, versions, q_count, kv_count, tile, *refs):
    (fixed, q_refs, kv_refs, t_refs, x_refs, outs, scratch), _ = taken(
        refs, (9, q_count, kv_count, terms, versions, 4, 4)
    )
    marks_ref, q_starts, kv_starts, dq_ref, gh_ref, gain_ref, mg_ref, cos_ref, sin_ref = fixed
    gin_ref, gp_ref, n_ref, small_ref = outs
    wq_ref, wkv_ref, q_sem, kv_sem = scratch
    tiles = [
        (wq_ref, k, copies)
        for k, copies in enumerate(weight_copies(q_starts, q_refs, wq_ref, q_sem, tile))
    ]
    tiles += [
        (wkv_ref, k, copies)
        for k, copies in enumerate(weight_copies(kv_starts, kv_refs, wkv_ref, kv_sem, tile))
    ]
    dkv = sum_refs(t_refs)
    cos = repeat_rows(cos_ref[...], reps)
    sin = repeat_rows(sin_ref[...], reps)
    parts = [
        turn(dkv[:, j * HEAD_DIM : (j + 1) * HEAD_DIM], cos, -sin) for j in range(KV_HEADS)
    ]
    parts.append(dkv[:, KCOLS:])
    gp_ref[:, :QCOLS] = dq_ref[...]
    gp_ref[:, QCOLS:] = jnp.concatenate(parts, axis=1).astype(bf16)
    grad_projected = gp_ref[...]
    width = gh_ref.shape[1]
    columns = gp_ref.shape[1]
    small_ref[:, width : width + columns] = jnp.sum(
        grad_projected.astype(f32), axis=0, keepdims=True
    )
    small_ref[:, width + columns :] = mg_ref[...]
    x = choose(marks_ref, x_refs).astype(f32)
    gain = gain_ref[...].astype(f32)
    n_ref[...] = (x * inverse_rms(x) * gain).astype(bf16)
    grad_normed = jnp.zeros(x.shape, f32)
    for at, (w_ref, k, copies) in enumerate(tiles):
        wait_all(copies)
        grad_normed = grad_normed + dot_nt(
            grad_projected[:, at * tile : (at + 1) * tile], w_ref[:, k * tile : (k + 1) * tile]
        )
    grad_source, grad_gain = norm_backward(grad_normed, x, gain)
    small_ref[:, :width] = grad_gain
    gin_ref[...] = (gh_ref[...] + grad_source).astype(bf16)


def project_back(marks, dq, xs, gh, gain, grad_mlp_gain, q_weight, kv_weight, cos, sin, terms, reps):
    q_pieces, q_starts = q_weight
    kv_pieces, kv_starts = kv_weight
    tokens, width = gh.shape
    columns = QCOLS + 2 * KCOLS
    tile = 2 * KCOLS
    weights = [far(w) for w in (*q_pieces, *kv_pieces)]
    return call(
        functools.partial(
            project_back_kernel, len(terms), reps, len(xs), len(q_pieces), len(kv_pieces), tile
        ),
        (
            jax.ShapeDtypeStruct((tokens, width), bf16),
            jax.ShapeDtypeStruct((tokens, columns), bf16),
            jax.ShapeDtypeStruct((tokens, width), bf16),
            jax.ShapeDtypeStruct((1, columns + 2 * width), f32),
        ),
        (marks, q_starts, kv_starts, dq, gh, gain, grad_mlp_gain, cos, sin, *weights, *terms, *xs),
        2 * tokens * width * columns,
        2 * width * columns,
        "project_back",
        limit=20,
        in_specs=[SMEM] * 3 + [VMEM] * 6 + [ANY] * len(weights) + [VMEM] * (len(terms) + len(xs)),
        out_specs=(VMEM,) * 4,
        scratch_shapes=[
            pltpu.VMEM((width, QCOLS), bf16),
            pltpu.VMEM((width, 2 * KCOLS), bf16),
            pltpu.SemaphoreType.DMA((QCOLS // tile, len(q_pieces))),
            pltpu.SemaphoreType.DMA((2 * KCOLS // tile, len(kv_pieces))),
        ],
    )


def add_kernel(parts, first, rows, *refs):
    outs = refs[len(refs) - parts :]
    total = refs[0][first : first + rows, :].astype(f32)
    for ref in refs[1 : len(refs) - parts]:
        total = total + ref[first : first + rows, :].astype(f32)
    total = total.astype(bf16)
    rows = rows // parts
    for k, out in enumerate(outs):
        out[...] = total[k * rows : (k + 1) * rows]


def add_up(terms, first, rows, parts=1, after=()):
    width = terms[0].shape[1]
    out = jax.ShapeDtypeStruct((rows // parts, width), bf16)
    return call(
        functools.partial(add_kernel, parts, first, rows),
        (out,) * parts,
        terms,
        0,
        2 * (len(terms) + 1) * rows * width,
        "add_up",
        limit=8,
        in_specs=[VMEM] * len(terms),
        after=after,
        out_specs=(VMEM,) * parts,
    )


def join_kernel(*refs):
    fill(refs[-1], refs[:-1])


def join(blocks):
    rows, width = blocks[0].shape
    return call(
        join_kernel,
        jax.ShapeDtypeStruct((rows * len(blocks), width), bf16),
        blocks,
        0,
        4 * len(blocks) * rows * width,
        "join",
        limit=4,
        in_specs=[VMEM] * len(blocks),
        out_specs=VMEM,
    )


def select_kernel(marks_ref, early_ref, late_ref, out_ref):
    out_ref[...] = choose(marks_ref, (early_ref, late_ref))


def select(marks, early, late):
    return call(
        select_kernel,
        jax.ShapeDtypeStruct(early.shape, early.dtype),
        (marks, early, late),
        0,
        6 * early.size,
        "select",
        limit=4,
        in_specs=[SMEM, VMEM, VMEM],
        out_specs=VMEM,
    )


def rows_kernel(at_ref, source, out, sem):
    rows = out.shape[0]
    at = pl.multiple_of(at_ref[0] * rows, ROWS)
    copy = pltpu.make_async_copy(source.at[pl.ds(at, rows)], out, sem)
    copy.start()
    copy.wait()


def rows_of(array, block, rows, after):
    out = jax.ShapeDtypeStruct((rows, array.shape[1]), array.dtype)
    return call(
        rows_kernel,
        out,
        (block.astype(jnp.int32).reshape(1), far(array)),
        0,
        4 * out.size,
        "rows_of",
        limit=4,
        in_specs=[SMEM, ANY],
        after=after,
        ordered=False,
        out_specs=VMEM,
        scratch_shapes=[pltpu.SemaphoreType.DMA(())],
    )


def collect_kernel(versions, *refs):
    (marks, outs, scratch) = refs[0], refs[-2], refs[-1]
    sources = refs[1:-2]
    count = len(sources) // versions
    rows = sources[0].shape[0]
    wait_all(
        bring(
            marks,
            [sources[k * versions : (k + 1) * versions] for k in range(count)],
            [outs.at[pl.ds(k * rows, rows)] for k in range(count)],
            scratch,
        )
    )


def collect(marks, early, late, after=()):
    count = len(early)
    rows, width = early[0].shape
    arrays = [a for pair in zip(early, late) for a in pair]
    return call(
        functools.partial(collect_kernel, 2),
        jax.ShapeDtypeStruct((count * rows, width), early[0].dtype),
        (marks, *arrays),
        0,
        4 * count * rows * width,
        "collect",
        limit=4,
        ordered=False,
        after=after,
        in_specs=[SMEM] + [ANY] * len(arrays),
        out_specs=ANY,
        scratch_shapes=[pltpu.SemaphoreType.DMA((count,))],
    )


def attention_grads_kernel(steps, versions, parts, *refs):
    (flags, small_refs, sources, outs, scratch), _ = taken(
        refs, (1, steps, 3 * steps + sum(versions), parts + 1, 5)
    )
    at_ref = flags[0]
    *outs, small_ref = outs
    n_ref, p_ref, a_ref, h_ref, sem = scratch
    size = n_ref.shape[0] // steps
    copies = []
    groups = []
    targets = []
    for k, target in enumerate((n_ref, p_ref, h_ref)):
        for t in range(steps):
            groups.append((sources[k * steps + t],))
            targets.append(target.at[pl.ds(t * size, size)])
    at = 3 * steps
    for t in range(steps):
        groups.append(sources[at : at + versions[t]])
        targets.append(a_ref.at[pl.ds(t * size, size)])
        at += versions[t]
    copies = bring(at_ref, groups, targets, sem)
    small_ref[...] = sum_refs(small_refs)
    wait_all(copies)
    columns = p_ref.shape[1]
    rows = outs[0].shape[0]
    for r, out in enumerate(outs):
        here = pl.ds(pl.multiple_of(at_ref[1 + r] * rows, HEAD_DIM), rows)
        out[:, :columns] = dot_tn(n_ref[:, here], p_ref[...]).astype(bf16)
        out[:, columns:] = dot_tn(a_ref[:, here], h_ref[...]).astype(bf16)


def attention_grads(marks, smalls, normed, projected, grad_hidden, attended, parts):
    steps = len(normed)
    tokens, width = normed[0].shape
    columns = projected[0].shape[1]
    rows = width // parts
    versions = [len(a) for a in attended]
    arrays = [*normed, *projected, *grad_hidden, *(a for item in attended for a in item)]
    total = steps * tokens
    return call(
        functools.partial(attention_grads_kernel, steps, versions, parts),
        (
            *(jax.ShapeDtypeStruct((rows, columns + width), bf16),) * parts,
            jax.ShapeDtypeStruct(smalls[0].shape, f32),
        ),
        (marks, *smalls, *arrays),
        2 * total * width * (columns + width),
        2 * total * (2 * width + columns) + 2 * width * (width + columns),
        "attention_grads",
        limit=40,
        in_specs=[SMEM] + [VMEM] * steps + [ANY] * len(arrays),
        out_specs=(VMEM,) * (parts + 1),
        scratch_shapes=[
            pltpu.VMEM((total, width), bf16),
            pltpu.VMEM((total, columns), bf16),
            pltpu.VMEM((total, width), bf16),
            pltpu.VMEM((total, width), bf16),
            pltpu.SemaphoreType.DMA((4 * steps,)),
        ],
    )


def assemble_kernel(pieces, *refs):
    at_ref = refs[0]
    piece_refs = refs[1 : 1 + pieces]
    left_ref, right_ref = refs[-2:]
    columns = left_ref.shape[1]
    rows = piece_refs[0].shape[0]
    for a, piece in enumerate(piece_refs):
        here = pl.ds(pl.multiple_of(at_ref[a] * rows, 8), rows)
        left_ref[here, :] = piece[:, :columns].astype(f32)
        right_ref[here, :] = piece[:, columns:].astype(f32)


def assemble(places, pieces, columns, after):
    rows, total = pieces[0].shape
    count = len(pieces)
    return call(
        functools.partial(assemble_kernel, count),
        (
            jax.ShapeDtypeStruct((rows * count, columns), f32),
            jax.ShapeDtypeStruct((rows * count, total - columns), f32),
        ),
        (places, *pieces),
        0,
        6 * rows * count * total,
        "assemble",
        limit=24,
        in_specs=[SMEM] + [VMEM] * count,
        after=after,
        ordered=False,
        out_specs=(VMEM, VMEM),
    )


def unit_tile(units, most):
    return max(t for t in range(16, most + 1, 16) if units % t == 0)


def weight_grad_kernel(aliased, adds, *refs):
    n_ref, g_ref, gate_ref, up_ref, down_ref = refs[:5]
    olds = refs[5 : 5 + aliased]
    news = refs[-4:-1]
    refs[-1][...] = jnp.zeros_like(refs[-1])

    @pl.when(pl.program_id(1) == 0)
    def _():
        for k, new in enumerate(news):
            new[...] = olds[k][...] if adds else jnp.zeros_like(new)

    rows = n_ref[...]
    grads = g_ref[...]
    gate_pre = dot_nt(gate_ref[...], rows)
    up_pre = dot_nt(up_ref[...], rows)
    grad_act = dot_nt(down_ref[...], grads)
    silu, grad_gate, grad_up = swiglu_backward(gate_pre, up_pre, grad_act)
    activated = (silu * up_pre).astype(bf16)
    news[0][...] += dot_nn(grad_gate, rows)
    news[1][...] += dot_nn(grad_up, rows)
    news[2][...] += dot_nn(activated, grads)


def weight_grads(n_all, g_all, gate, up, down, outs, adds, first, count, after):
    units, width = gate.shape
    tokens = n_all.shape[0]
    tile = unit_tile(units, 320)
    chunk = math.gcd(tokens, 1024)
    shape = jax.ShapeDtypeStruct((units, width), f32)
    part = pl.BlockSpec((tile, width), lambda i, j: (i + first, 0))
    rows = pl.BlockSpec((chunk, width), lambda i, j: (j, 0))
    *outs, zeros = call(
        functools.partial(weight_grad_kernel, len(outs), adds),
        (*(shape,) * 3, jax.ShapeDtypeStruct((8, 128), f32)),
        (n_all, g_all, gate, up, down, *outs),
        12 * tokens * width * tile * count,
        18 * width * tile * count,
        "weight_grads",
        limit=60,
        ordered=False,
        grid=(count, tokens // chunk),
        in_specs=[rows] * 2
        + [part] * 3
        + [part if adds else ANY] * len(outs),
        after=after,
        out_specs=((*(part,) * 3, pl.BlockSpec((8, 128), lambda i, j: (0, 0)))),
        input_output_aliases={len(after) + 5 + k: k for k in range(len(outs))},
    )
    return outs, zeros


def body(
    inputs,
    cotangent,
    attn_gain,
    qkv_weight,
    qkv_bias,
    out_weight,
    mlp_gain,
    gate_weight,
    up_weight,
    down_weight,
):
    first = lax.axis_index("section") == 0
    micro, rows_here, _, width = inputs.shape
    fsdp = lax.axis_size("fsdp")
    ctx = lax.axis_size("ctx")
    fsdp_at = lax.axis_index("fsdp")
    ctx_at = lax.axis_index("ctx")
    tokens = 2 * rows_here
    reps = MICROS
    chunks = micro // reps
    steps = chunks + LAG
    span_rows = rows_here * fsdp
    half_rows = span_rows * ctx

    def places_of(c, f, token):
        index = (c * fsdp + f) * rows_here + token // 2
        second = 2 * half_rows - span_rows * (index // span_rows + 1) + index % span_rows
        return jnp.where(token % 2 == 0, index, second)

    own = places_of(ctx_at, fsdp_at, jnp.arange(tokens, dtype=jnp.int32))
    shape = (fsdp, tokens, ctx * tokens)
    number = lax.broadcasted_iota(jnp.int32, shape, 0)
    other = jnp.zeros(shape, jnp.int32)
    for k, r in enumerate(relative_order(fsdp)):
        other = jnp.where(number == k, fsdp_at ^ r, other)
    column = lax.broadcasted_iota(jnp.int32, shape, 2)
    key_places = places_of(ctx_at ^ (column // tokens), other, column % tokens)
    query_places = places_of(ctx_at, fsdp_at, lax.broadcasted_iota(jnp.int32, shape, 1))
    mask = jnp.where(key_places <= query_places, 0.0, NEGATIVE).astype(f32)
    half = HEAD_DIM // 2
    frequency = ROPE_BASE ** (-(jnp.arange(half, dtype=f32) * 2.0) / HEAD_DIM)
    angles = own.astype(f32)[:, None] * frequency
    cos = jnp.concatenate([jnp.cos(angles)] * 2, axis=1)
    sin = jnp.concatenate([-jnp.sin(angles), jnp.sin(angles)], axis=1)

    packed = jnp.concatenate([attn_gain, qkv_bias, mlp_gain], axis=1)
    packed_pieces = gather_pieces(packed, "fsdp")
    owners = jnp.arange(fsdp, dtype=jnp.int32)[:, None]
    packed = functools.reduce(
        jnp.add,
        [
            jnp.where(owners == fsdp_at ^ r, piece, jnp.zeros_like(piece))
            for r, piece in zip(relative_order(fsdp), packed_pieces)
        ],
    )
    gain_part, bias_part = attn_gain.shape[1], qkv_bias.shape[1]
    attn_full = packed[:, :gain_part].reshape(1, -1)
    bias_full = packed[:, gain_part : gain_part + bias_part].reshape(1, -1)
    mlp_full = packed[:, gain_part + bias_part :].reshape(1, -1)

    def gathered(shard, after=None):
        units = shard.shape[0] // ROWS
        pieces = [(shard, fsdp_at * units)]
        for bit in bits_of(fsdp):
            if len(pieces) == 1 and after is not None:
                half = units // 2
                odd = ctx_at & 1
                mine = exchange(rows_of(shard, odd, half * ROWS, after), "fsdp", bit)
                other = exchange(mine, "ctx", 1)
                base = (fsdp_at ^ bit) * units
                pieces += [(mine, base + odd * half), (other, base + (1 - odd) * half)]
            else:
                pieces += [
                    (exchange(piece, "fsdp", bit), (at // units ^ bit) * units + at % units)
                    for piece, at in pieces
                ]
        starts = jnp.stack([at.astype(jnp.int32) for _, at in pieces])
        return [piece for piece, _ in pieces], starts

    kv_weight = gathered(qkv_weight[0, :, QCOLS:])
    q_weight = gathered(qkv_weight[0, :, :QCOLS], kv_weight[0][1:2])
    gate, up, down = gate_weight[0], up_weight[0], down_weight[0]
    flag = first.astype(jnp.int32)
    marks = jnp.stack([flag] + [(fsdp_at ^ r).astype(jnp.int32) for r in relative_order(fsdp)])

    def chunked(array):
        return array.reshape(chunks, reps * tokens, width)

    in_chunks = chunked(inputs)
    cot_chunks = chunked(cotangent)

    def pick(early, late):
        return jnp.where(first, early, late)

    def versions(u, early, late):
        if u < LAG:
            return (late[u + LAG],)
        if u < chunks:
            return (early[u - LAG], late[u + LAG])
        return (early[u - LAG],)

    gys = [jnp.where(first, jnp.zeros_like(cot), cot) for cot in cot_chunks[:LAG]]
    early_pieces = [gather_pieces(gy, "fsdp") for gy in gys]
    gys = dict(enumerate(gys))

    ORDER.clear()

    def pick(early, late):
        return jnp.where(first, early, late)

    def versions(u, early, late):
        if u < LAG:
            return (late[u + LAG],)
        if u < chunks:
            return (early[u - LAG], late[u + LAG])
        return (early[u - LAG],)


    first_keys, out_weights = [], []
    near_weights = [gate, up, down]
    outputs, moved, xs, kept, attended, n2_pieces = {}, {}, {}, {}, {}, {}
    grads_in, grads_moved, smalls, factors = {}, {}, {}, {}

    def add_one(terms, rows):
        return add_up(terms, rows, rows)[0]

    def forward(t):
        if t < LAG:
            x = (in_chunks[t],)
        elif t < chunks:
            x = (in_chunks[t], moved[t])
        else:
            x = (moved[t],)
        xs[t] = x
        kv = project(
            marks, x, attn_full, kv_weight, bias_full[:, QCOLS:], cos, sin, reps, KV_HEADS
        )
        first_keys.append(kv)
        blocks = [kv] + [exchange(kv, "ctx", a) for a in range(1, ctx)]
        yield "K"
        for name in "QJ" if LAG <= t < chunks else "JQ":
            if name == "J":
                kv_pieces = gather_pieces(join(blocks), "fsdp")
            else:
                q = project(
                    marks, x, attn_full, q_weight, bias_full[:, :QCOLS], cos, sin, reps, HEADS
                )
            yield name
        if t == 0:
            out_weights.extend(gathered(out_weight[0], first_keys))
        after = [p for pieces in early_pieces for p in pieces[1:]] if t == LAG else []
        att, hidden, n2 = attend(
            marks, q, x, mask, out_weights, mlp_full, kv_pieces, reps, after
        )
        attended[t] = att
        n2_pieces[t] = gather_pieces(n2, "fsdp")
        kept[t] = (hidden, q, *kv_pieces)
        yield "A"
        parts = mlp(n2_pieces[t], *near_weights)
        terms = yield from stages(reduction(*parts, "fsdp", add_one), "M", "R")
        outputs[t] = add_up([hidden, *terms], 0, hidden.shape[0])[0]
        if t < chunks:
            moved[t + LAG] = passed_along(outputs[t], "section", 1)
        yield "Y"

    def stages(generator, first_name, name):
        while True:
            try:
                next(generator)
            except StopIteration as end:
                return end.value
            yield first_name
            first_name = name

    def backward(u):
        if u < LAG:
            gy, g_pieces = gys[u], early_pieces[u]
        else:
            gy = select(marks, grads_moved[u], cot_chunks[u]) if u < chunks else grads_moved[u]
            gys[u] = gy
            g_pieces = gather_pieces(gy, "fsdp")
            yield "G"
        n2_now = list(zip(*versions(u, n2_pieces, n2_pieces)))
        parts = mlp_back(marks, n2_now, g_pieces, *near_weights, [])
        terms = yield from stages(reduction(*parts, "fsdp", add_one), "B", "S")
        kept_now = list(zip(*versions(u, kept, kept)))
        gh, gh_low, dq, grad_mlp_gain, *dkv = attend_back(
            marks, gy, mlp_full, out_weights, mask, cos, sin, terms, kept_now, reps
        )
        terms = yield from stages(reduction(*dkv, "fsdp", add_one), "T", "D")
        own, *others = add_up(terms, 0, ctx * reps * tokens, ctx)
        dkv_terms = [own] + [exchange(other, "ctx", a + 1) for a, other in enumerate(others)]
        yield "E"
        x_now = versions(u, {t: x[0] for t, x in xs.items()}, {t: x[-1] for t, x in xs.items()})
        g_in, g_proj, normed, small = project_back(
            marks,
            dq,
            x_now,
            gh,
            attn_full,
            grad_mlp_gain,
            q_weight,
            kv_weight,
            cos,
            sin,
            dkv_terms,
            reps,
        )
        grads_in[u] = g_in
        if u < chunks:
            grads_moved[u + LAG] = passed_along(g_in, "section", -1)
        smalls[u] = small
        factors[u] = (normed, g_proj, gh_low, versions(u, attended, attended))
        yield "P"

    running = {}
    for name in SEQUENCE.split():
        if name == "H":
            near_weights[:] = hold(gate, up, down)
            continue
        kind, step = name[0], int(name[1:])
        key = (kind in FORWARD, step)
        if key not in running:
            running[key] = forward(step) if key[0] else backward(step)
        while next(running[key]) != kind:
            pass
    grads_in, gys, smalls, factors = (
        [found[t] for t in range(steps)] for found in (grads_in, gys, smalls, factors)
    )

    batches = [b for b in (range(0, chunks // 2), range(chunks // 2, chunks)) if len(b)]

    def all_tokens(early, late, batch):
        own_rows = collect(marks, [early[m] for m in batch], [late[m] for m in batch])
        return lax.all_gather(own_rows, ("ctx", "fsdp"), axis=0, tiled=True)

    n2_own = [n2_pieces[t][0] for t in range(steps)]
    n2_all = [all_tokens(n2_own, n2_own[LAG:], batch) for batch in batches]
    g_all = [all_tokens(gys[LAG:], gys, batch) for batch in batches]
    tiles = gate.shape[0] // unit_tile(gate.shape[0], 320)
    cuts = [0, tiles // 7, 6 * tiles // 7, tiles], [0, 3 * tiles // 7, tiles]
    plan = [
        (b, i, j - i)
        for b in range(len(batches))
        for i, j in zip(cuts[b], cuts[b][1:])
        if j > i
    ]
    mlp_grads = []

    def some_weight_grads(after):
        nonlocal mlp_grads
        if not plan:
            return None
        b, start, count = plan.pop(0)
        mlp_grads, zeros = weight_grads(
            n2_all[b], g_all[b], gate, up, down, mlp_grads, b > 0, start, count, after
        )
        return zeros

    lead = QCOLS + KCOLS
    columns = QCOLS + 2 * KCOLS
    normed, projected, grad_hidden, att_now = zip(*factors)
    rows = width // fsdp
    if rows % HEAD_DIM == 0:
        *summed, small = attention_grads(
            marks, smalls, normed, projected, grad_hidden, att_now, fsdp
        )
    else:
        start = jnp.stack([flag, jnp.int32(0)])
        large, small = attention_grads(
            start, smalls, normed, projected, grad_hidden, att_now, 1
        )
        summed = [
            lax.dynamic_slice_in_dim(large, (fsdp_at ^ r) * rows, rows)
            for r in relative_order(fsdp)
        ]
    small = small.reshape(-1, HEAD_DIM)
    for bit in reversed(bits_of(fsdp)):
        count = len(summed) // 2
        moves = [exchange(p, "fsdp", bit) for p in summed[count:]]
        zeros = some_weight_grads(summed[:1])
        zero = 0.0 if zeros is None else zeros[0, 0]
        small = small + zero
        summed = [
            (p.astype(f32) + m.astype(f32) + zero).astype(bf16) for p, m in zip(summed, moves)
        ]
        small = small + exchange(small, "fsdp", bit)
    rows = width // fsdp // ctx
    terms = [
        lax.dynamic_slice_in_dim(summed[0], (ctx_at ^ a) * rows, rows) for a in range(ctx)
    ]
    moves = [exchange(terms[a], "ctx", a) for a in range(1, ctx)]
    small = small + exchange(small, "ctx", bits_of(ctx)[0])
    zeros = some_weight_grads(terms[:1])
    zeros = some_weight_grads([]) if plan else zeros
    block = functools.reduce(jnp.add, [t.astype(f32) for t in (terms[0], *moves)])
    small = small + (0.0 if zeros is None else zeros[0, 0])
    block = (block + (0.0 if zeros is None else zeros[0, 0])).astype(bf16)
    pieces = [block] + [exchange(block, "ctx", a) for a in range(1, ctx)]
    for bit in bits_of(ctx)[1:]:
        small = small + exchange(small, "ctx", bit)
    zeros = some_weight_grads([block])
    places = jnp.stack([(ctx_at ^ a).astype(jnp.int32) for a in range(ctx)])
    ends = [] if zeros is None else [zeros]
    grad_qkv, grad_out = assemble(places, pieces, columns, [] if zeros is None else [zeros])
    while plan:
        some_weight_grads([])
    grad_gate, grad_up, grad_down = mlp_grads

    small = small.reshape(-1)

    def cut(start, length):
        part = length // fsdp
        return lax.dynamic_slice(small, (start + fsdp_at * part,), (part,))

    grad_attn_gain = cut(0, width)
    grad_bias_lead = cut(width, lead)
    grad_bias_value = cut(width + lead, columns - lead)
    grad_mlp_gain = cut(width + columns, width)

    for generator in running.values():
        for _ in generator:
            pass
    outputs = [outputs[t] for t in range(steps)]
    layer_outputs = collect(marks, outputs[:chunks], outputs[LAG:], ends).reshape(inputs.shape)
    input_grads = collect(marks, grads_in[LAG:], grads_in[:chunks], ends).reshape(inputs.shape)
    return (
        layer_outputs[None],
        input_grads[None],
        grad_attn_gain[None],
        grad_qkv[None],
        grad_bias_lead[None],
        grad_bias_value[None],
        grad_out[None],
        grad_mlp_gain[None],
        grad_gate[None],
        grad_up[None],
        grad_down[None],
    )


def solution(mesh):
    rows = P(None, ("ctx", "fsdp"), None, None)
    vector = P("section", "fsdp")
    matrix = P("section", "fsdp", None)
    stacked = P("section", None, ("ctx", "fsdp"), None, None)
    in_specs = (rows, rows, vector, matrix, vector, matrix, vector, matrix, matrix, matrix)
    out_specs = (
        stacked,
        stacked,
        vector,
        matrix,
        vector,
        vector,
        matrix,
        vector,
        matrix,
        matrix,
        matrix,
    )
    return jax.shard_map(body, mesh=mesh, in_specs=in_specs, out_specs=out_specs, check_vma=False)
```

```python
import functools
import math

import jax
import jax.numpy as jnp
from jax import lax
from jax.experimental import pallas as pl
from jax.experimental.pallas import tpu as pltpu
from jax.sharding import PartitionSpec as P

HEADS = 12
KV_HEADS = 2
HEAD_DIM = 128
GROUP = HEADS // KV_HEADS
EPS = 1e-06
ROPE_BASE = 1000000.0
NEGATIVE = -1e30
QCOLS = HEADS * HEAD_DIM
KCOLS = KV_HEADS * HEAD_DIM
SCALE = HEAD_DIM ** (-0.5)

MICROS = 2
LAG = 1
FORWARD = "KJQAMRY"
SEQUENCE = (
    "K0", "J0", "Q0", "A0", "H", "M0", "R0", "Y0", "K1", "Q1", "J1", "A1",
    "H", "M1", "R1", "B0", "Y1", "S0", "K2", "T0", "D0", "J2", "Q2", "E0",
    "P0", "A2", "G1", "H", "B1", "S1", "T1", "D1", "E1", "P1", "G2", "H",
    "B2", "M2", "S2", "T2", "D2", "E2", "P2",
)
ROWS = 16
UNITS = 512

f32 = jnp.float32
bf16 = jnp.bfloat16
MIB = 1 << 20


def dot_nn(a, b):
    return lax.dot_general(a, b, (((1,), (0,)), ((), ())), preferred_element_type=f32)


def dot_nt(a, b):
    return lax.dot_general(a, b, (((1,), (1,)), ((), ())), preferred_element_type=f32)


def dot_tn(a, b):
    return lax.dot_general(a, b, (((0,), (0,)), ((), ())), preferred_element_type=f32)


def inverse_rms(values):
    return lax.rsqrt(jnp.mean(values * values, axis=-1, keepdims=True) + EPS)


def norm_backward(grad_normed, values, gain):
    inverse = inverse_rms(values)
    scaled = grad_normed * gain
    grad_values = inverse * scaled - values * (
        inverse**3 * jnp.mean(scaled * values, axis=-1, keepdims=True)
    )
    grad_gain = jnp.sum(grad_normed * values * inverse, axis=0, keepdims=True)
    return grad_values, grad_gain


def exchange(block, axis, mask):
    size = lax.axis_size(axis)
    return lax.ppermute(block, axis, [(i, i ^ mask) for i in range(size)])


def passed_along(block, axis, distance):
    devices = range(lax.axis_size(axis))
    route = [(i - distance, i) for i in devices if i - distance in devices]
    return lax.ppermute(block, axis, route)


def bits_of(size):
    return [1 << b for b in reversed(range(size.bit_length() - 1))]


def relative_order(size):
    order = [0]
    for bit in bits_of(size):
        order = order + [r ^ bit for r in order]
    return order


def gather_pieces(block, axis):
    pieces = [block]
    for bit in bits_of(lax.axis_size(axis)):
        pieces = pieces + [exchange(p, axis, bit) for p in pieces]
    return pieces


def reduction(near, far_half, axis, total):
    terms = [near]
    sent = far_half
    extent = near.shape[0]
    bits = bits_of(lax.axis_size(axis))[::-1]
    for k, bit in enumerate(bits):
        if k > 0:
            extent //= 2
            sent = total(terms, extent)
        terms.append(exchange(sent, axis, bit))
        yield
    return terms


ORDER = []


def call(
    kernel, out_shape, args, flops, moved, name, in_specs, limit=24, after=(), ordered=True, **kwargs
):
    waits = [*after, *(ORDER if ordered else ())]

    def body(*refs):
        kernel(*refs[len(waits) :])

    result = pl.pallas_call(
        body,
        out_shape=out_shape,
        in_specs=[*[ANY] * len(waits), *in_specs],
        compiler_params=pltpu.CompilerParams(vmem_limit_bytes=limit * MIB),
        cost_estimate=pl.CostEstimate(flops=flops, bytes_accessed=moved, transcendentals=0),
        name=name,
        **kwargs,
    )(*waits, *args)
    if ordered:
        ORDER[:] = [result[0] if isinstance(result, (tuple, list)) else result]
    return result


ANY = pl.BlockSpec(memory_space=pl.ANY)
VMEM = pl.BlockSpec(memory_space=pltpu.VMEM)
SMEM = pl.BlockSpec(memory_space=pltpu.SMEM)


def hold_kernel(count, *refs):
    copies = [
        pltpu.make_async_copy(refs[k], refs[count + k], refs[-1].at[k]) for k in range(count)
    ]
    for copy in copies:
        copy.start()
    wait_all(copies)


def hold(*arrays):
    return call(
        functools.partial(hold_kernel, len(arrays)),
        tuple(pltpu.VMEM(a.shape, a.dtype) for a in arrays),
        [far(a) for a in arrays],
        0,
        2 * sum(a.size for a in arrays),
        "hold",
        limit=4,
        in_specs=[ANY] * len(arrays),
        out_specs=tuple(VMEM for _ in arrays),
        scratch_shapes=[pltpu.SemaphoreType.DMA((len(arrays),))],
    )


def held(array):
    return pltpu.with_memory_space_constraint(array, pltpu.VMEM)


def far(array):
    return pltpu.with_memory_space_constraint(array, pltpu.HBM)


def bring(marks_ref, sources, targets, sem):
    copies = []
    for k, (source, target) in enumerate(zip(sources, targets)):
        if len(source) == 1:
            copy = pltpu.make_async_copy(source[0], target, sem.at[k])
            copy.start()
        else:
            for is_first, ref in zip((1, 0), source):
                copy = pltpu.make_async_copy(ref, target, sem.at[k])
                pl.when(marks_ref[0] == is_first)(copy.start)
        copies.append(copy)
    return copies


def taken(refs, counts):
    groups = []
    for count in counts:
        groups.append(refs[:count])
        refs = refs[count:]
    return groups, refs


def turn(value, cos, sin):
    return value * cos + pltpu.roll(value, HEAD_DIM // 2, 1) * sin


def repeat_rows(table, count):
    return table if count == 1 else jnp.concatenate([table] * count, axis=0)


def choose(marks_ref, refs):
    if len(refs) == 1:
        return refs[0][...]
    return jnp.where(marks_ref[0] == 1, refs[0][...], refs[1][...])


def weight_copies(starts_ref, pieces, target, sem, tile=None):
    columns = target.shape[1]
    tile = tile or columns
    tiles = []
    for k in range(columns // tile):
        copies = []
        for r, piece in enumerate(pieces):
            at = pl.multiple_of(starts_ref[r] * ROWS, ROWS)
            there = target.at[pl.ds(at, piece.shape[0]), pl.ds(k * tile, tile)]
            copy = pltpu.make_async_copy(piece.at[:, pl.ds(k * tile, tile)], there, sem.at[k, r])
            copy.start()
            copies.append(copy)
        tiles.append(copies)
    return tiles


def wait_all(copies):
    for copy in copies:
        copy.wait()


def project_kernel(reps, versions, pieces, turned_heads, tile, *refs):
    (fixed, w_refs, x_refs), rest = taken(refs, (6, pieces, versions))
    marks_ref, starts_ref, gain_ref, b_ref, cos_ref, sin_ref = fixed
    out_ref, n_ref, w_ref, sem = rest[-4:]
    tiles = weight_copies(starts_ref, w_refs, w_ref, sem, tile)
    x = choose(marks_ref, x_refs).astype(f32)
    n_ref[...] = (x * inverse_rms(x) * gain_ref[...].astype(f32)).astype(bf16)
    cos = repeat_rows(cos_ref[...], reps)
    sin = repeat_rows(sin_ref[...], reps)
    for k, copies in enumerate(tiles):
        here = slice(k * tile, (k + 1) * tile)
        wait_all(copies)
        projected = dot_nn(n_ref[...], w_ref[:, here]) + b_ref[:, here].astype(f32)
        turned = []
        for j in range(tile // HEAD_DIM):
            part = projected[:, j * HEAD_DIM : (j + 1) * HEAD_DIM]
            head = k * tile // HEAD_DIM + j
            turned.append(turn(part, cos, sin) if head < turned_heads else part)
        out_ref[:, here] = jnp.concatenate(turned, axis=1).astype(bf16)


def project(marks, xs, gain, weight, b, cos, sin, reps, turned_heads, after=()):
    w_pieces, starts = weight
    tokens, width = xs[0].shape
    columns = w_pieces[0].shape[1]
    tile = 2 * KCOLS
    count = len(w_pieces)
    return call(
        functools.partial(project_kernel, reps, len(xs), count, turned_heads, tile),
        jax.ShapeDtypeStruct((tokens, columns), bf16),
        (marks, starts, gain, b, cos, sin, *(far(w) for w in w_pieces), *xs),
        2 * tokens * width * columns,
        2 * width * columns,
        "project",
        limit=16,
        in_specs=[SMEM] * 2 + [VMEM] * 4 + [ANY] * count + [VMEM] * len(xs),
        after=after,
        out_specs=VMEM,
        scratch_shapes=[
            pltpu.VMEM((tokens, width), bf16),
            pltpu.VMEM((width, columns), bf16),
            pltpu.SemaphoreType.DMA((columns // tile, count)),
        ],
    )


def head_rows(block, g):
    return jnp.concatenate(
        [
            block[:, (g * GROUP + j) * HEAD_DIM : (g * GROUP + j + 1) * HEAD_DIM]
            for j in range(GROUP)
        ],
        axis=0,
    )


def head_columns(rows, tokens):
    return [rows[j * tokens : (j + 1) * tokens] for j in range(GROUP)]


def key_rows(ref, seq, reps, tokens, column):
    columns = slice(column * HEAD_DIM, (column + 1) * HEAD_DIM)
    if reps == 1:
        return ref[:, columns]
    stride = reps * tokens
    return jnp.concatenate(
        [
            ref[a * stride + seq * tokens : a * stride + (seq + 1) * tokens, columns]
            for a in range(ref.shape[0] // stride)
        ],
        axis=0,
    )


def masked_scores(q, key_block, mask, tokens):
    scores = dot_nt(q, key_block) * SCALE
    keys = scores.shape[1]
    return (scores.reshape(GROUP, tokens, keys) + mask[None]).reshape(GROUP * tokens, keys)


def attend_kernel(pieces, weights, reps, versions, *refs):
    (fixed, ow_refs, kv_refs, x_refs), rest = taken(refs, (5, weights, pieces, versions))
    marks_ref, starts_ref, q_ref, mask_ref, gain_ref = fixed
    att_ref, hid_ref, n2_ref, ow_ref, sem = rest[-5:]
    (weights_in,) = weight_copies(starts_ref, ow_refs, ow_ref, sem)
    tokens = q_ref.shape[0] // reps
    for seq in range(reps):
        rows = slice(seq * tokens, (seq + 1) * tokens)
        q_all = q_ref[rows, :]
        for g in range(KV_HEADS):
            q = head_rows(q_all, g)
            scores = [
                masked_scores(q, key_rows(kv, seq, reps, tokens, g), mask_ref[p], tokens)
                for p, kv in enumerate(kv_refs)
            ]
            top = functools.reduce(
                jnp.maximum, [jnp.max(s, axis=-1, keepdims=True) for s in scores]
            )
            total = jnp.zeros_like(top)
            acc = jnp.zeros((GROUP * tokens, HEAD_DIM), f32)
            for s, kv in zip(scores, kv_refs):
                weights = jnp.exp(s - top)
                total = total + jnp.sum(weights, axis=-1, keepdims=True)
                acc = acc + dot_nn(
                    weights.astype(bf16), key_rows(kv, seq, reps, tokens, KV_HEADS + g)
                )
            low = (acc / total).astype(bf16)
            for j, block in enumerate(head_columns(low, tokens)):
                head = g * GROUP + j
                att_ref[rows, head * HEAD_DIM : (head + 1) * HEAD_DIM] = block
    wait_all(weights_in)
    hidden = choose(marks_ref, x_refs).astype(f32) + dot_nn(att_ref[...], ow_ref[...])
    hid_ref[...] = hidden
    n2_ref[...] = (hidden * inverse_rms(hidden) * gain_ref[...].astype(f32)).astype(bf16)


def attend(marks, q, xs, mask, weight, gain, kv_pieces, reps, after=()):
    ow_pieces, starts = weight
    tokens, width = xs[0].shape
    keys = sum(p.shape[0] for p in kv_pieces)
    return call(
        functools.partial(attend_kernel, len(kv_pieces), len(ow_pieces), reps, len(xs)),
        (
            jax.ShapeDtypeStruct((tokens, QCOLS), bf16),
            jax.ShapeDtypeStruct((tokens, width), f32),
            jax.ShapeDtypeStruct((tokens, width), bf16),
        ),
        (marks, starts, q, mask, gain, *(far(w) for w in ow_pieces), *kv_pieces, *xs),
        2 * tokens * QCOLS * width + 12 * tokens * QCOLS * keys // reps,
        4 * keys * KCOLS + 12 * tokens * width,
        "attend",
        limit=16 + 24 * keys // (reps * 4096),
        in_specs=[SMEM] * 2
        + [VMEM] * 3
        + [ANY] * len(ow_pieces)
        + [VMEM] * (len(kv_pieces) + len(xs)),
        after=after,
        out_specs=(VMEM,) * 3,
        scratch_shapes=[
            pltpu.VMEM((QCOLS, width), bf16),
            pltpu.SemaphoreType.DMA((1, len(ow_pieces))),
        ],
    )


def fill(scratch, refs):
    size = refs[0].shape[0]
    for p, ref in enumerate(refs):
        scratch[p * size : (p + 1) * size, :] = ref[...]


def spread(out_refs, acc_ref):
    fill_from = 0
    for ref in out_refs:
        ref[...] = acc_ref[fill_from : fill_from + ref.shape[0], :].astype(bf16)
        fill_from += ref.shape[0]


def unit_spans(units):
    return [slice(at, min(at + UNITS, units)) for at in range(0, units, UNITS)]


def mlp_kernel(pieces, *refs):
    n_refs = refs[:pieces]
    gate_ref, up_ref, down_ref = refs[pieces : pieces + 3]
    out_refs = refs[-4:-2]
    cat_ref, acc_ref = refs[-2:]
    fill(cat_ref, n_refs)
    for k, here in enumerate(unit_spans(gate_ref.shape[0])):
        rows = cat_ref[...]
        gate_pre = dot_nt(rows, gate_ref[here, :])
        up_pre = dot_nt(rows, up_ref[here, :])
        activated = (jax.nn.sigmoid(gate_pre) * gate_pre * up_pre).astype(bf16)
        term = dot_nn(activated, down_ref[here, :])
        if k == 0:
            acc_ref[...] = term
        else:
            acc_ref[...] += term
    spread(out_refs, acc_ref)


def mlp(n_pieces, gate, up, down, after=()):
    units, width = gate.shape
    tokens = n_pieces[0].shape[0]
    count = len(n_pieces)
    return call(
        functools.partial(mlp_kernel, count),
        (jax.ShapeDtypeStruct((count // 2 * tokens, width), bf16),) * 2,
        (*n_pieces, held(gate), held(up), held(down)),
        6 * count * tokens * width * units,
        4 * count * tokens * width,
        "mlp",
        limit=12 * max(1, count * tokens // 512),
        in_specs=[VMEM] * (count + 3),
        after=after,
        out_specs=(VMEM,) * 2,
        scratch_shapes=[
            pltpu.VMEM((count * tokens, width), bf16),
            pltpu.VMEM((count * tokens, width), f32),
        ],
    )


def swiglu_backward(gate_pre, up_pre, grad_act):
    sigmoid = jax.nn.sigmoid(gate_pre)
    silu = gate_pre * sigmoid
    grad_gate = (grad_act * up_pre * (sigmoid + silu * (1.0 - sigmoid))).astype(bf16)
    grad_up = (grad_act * silu).astype(bf16)
    return silu, grad_gate, grad_up


def mlp_back_kernel(pieces, versions, *refs):
    (flags, weights, n_refs, g_refs), rest = taken(
        refs, (1, 3, pieces * versions, pieces)
    )
    gate_ref, up_ref, down_ref = weights
    out_refs = rest[-6:-4]
    cat_ref, gcat_ref, acc_ref, sem = rest[-4:]
    size = cat_ref.shape[0] // pieces
    spans = [pl.ds(p * size, size) for p in range(pieces)]
    sources = [n_refs[p * versions : (p + 1) * versions] for p in range(pieces)]
    copies = bring(
        flags[0],
        sources + [(g,) for g in g_refs],
        [cat_ref.at[span] for span in spans] + [gcat_ref.at[span] for span in spans],
        sem,
    )
    for copy in copies:
        copy.wait()
    for k, here in enumerate(unit_spans(gate_ref.shape[0])):
        rows = cat_ref[...]
        gate_pre = dot_nt(rows, gate_ref[here, :])
        up_pre = dot_nt(rows, up_ref[here, :])
        grad_act = dot_nt(gcat_ref[...], down_ref[here, :])
        _, grad_gate, grad_up = swiglu_backward(gate_pre, up_pre, grad_act)
        term = dot_nn(grad_gate, gate_ref[here, :]) + dot_nn(grad_up, up_ref[here, :])
        if k == 0:
            acc_ref[...] = term
        else:
            acc_ref[...] += term
    spread(out_refs, acc_ref)


def mlp_back(flag, n_versions, g_pieces, gate, up, down, after):
    units, width = gate.shape
    tokens = g_pieces[0].shape[0]
    count = len(g_pieces)
    versions = len(n_versions[0])
    n_arrays = [far(array) for piece in n_versions for array in piece]
    return call(
        functools.partial(mlp_back_kernel, count, versions),
        (jax.ShapeDtypeStruct((count // 2 * tokens, width), bf16),) * 2,
        (flag, held(gate), held(up), held(down), *n_arrays, *g_pieces),
        10 * count * tokens * width * units,
        6 * count * tokens * width,
        "mlp_back",
        limit=16 * max(1, count * tokens // 512),
        in_specs=[SMEM] + [VMEM] * 3 + [ANY] * (len(n_arrays) + count),
        after=after,
        out_specs=(VMEM,) * 2,
        scratch_shapes=[
            pltpu.VMEM((count * tokens, width), bf16),
            pltpu.VMEM((count * tokens, width), bf16),
            pltpu.VMEM((count * tokens, width), f32),
            pltpu.SemaphoreType.DMA((2 * count,)),
        ],
    )


def sum_refs(refs, rows=None):
    rows = rows or refs[0].shape[0]
    total = refs[0][:rows, :].astype(f32)
    for ref in refs[1:]:
        total = total + ref[:rows, :].astype(f32)
    return total


def attend_back_kernel(pieces, weights, terms, reps, versions, *refs):
    (fixed, ow_refs, t_refs, sources, outs, dkv_refs, scratch), _ = taken(
        refs, (7, weights, terms, (2 + pieces) * versions, 4, 2, 6)
    )
    marks_ref, starts_ref, gy_ref, gain_ref, mask_ref, cos_ref, sin_ref = fixed
    gh_ref, ghl_ref, dq_ref, mg_ref = outs
    hid_ref, q_ref, kv_ref, sem, ow_ref, ow_sem = scratch
    kv_refs = [kv_ref.at[p] for p in range(pieces)]
    *copies, hidden_in = bring(
        marks_ref,
        [sources[k * versions : (k + 1) * versions] for k in (*range(1, 2 + pieces), 0)],
        [q_ref, *kv_refs, hid_ref],
        sem,
    )
    (weights_in,) = weight_copies(starts_ref, ow_refs, ow_ref, ow_sem)
    tokens = q_ref.shape[0] // reps
    wait_all(copies)
    places = [(seq, g) for seq in range(reps) for g in range(KV_HEADS)]
    probs_at = {}
    for seq, g in places:
        q = head_rows(q_ref[seq * tokens : (seq + 1) * tokens, :], g)
        scores = [
            masked_scores(q, key_rows(kv, seq, reps, tokens, g), mask_ref[p], tokens)
            for p, kv in enumerate(kv_refs)
        ]
        top = functools.reduce(jnp.maximum, [jnp.max(s, axis=-1, keepdims=True) for s in scores])
        weights = [jnp.exp(s - top) for s in scores]
        total = functools.reduce(jnp.add, [jnp.sum(w, axis=-1, keepdims=True) for w in weights])
        scale = 1.0 / total
        probs_at[seq, g] = [w * scale for w in weights]
    hidden_in.wait()
    grad_from_two, grad_gain = norm_backward(
        sum_refs(t_refs, hid_ref.shape[0]), hid_ref[...], gain_ref[...].astype(f32)
    )
    mg_ref[...] = grad_gain
    grad_hidden = gy_ref[...].astype(f32) + grad_from_two
    gh_ref[...] = grad_hidden
    grad_low = grad_hidden.astype(bf16)
    ghl_ref[...] = grad_low
    wait_all(weights_in)
    grad_att = dot_nt(grad_low, ow_ref[...]).astype(bf16)
    cos = cos_ref[...]
    sin = sin_ref[...]
    for seq, g in places:
        rows = slice(seq * tokens, (seq + 1) * tokens)
        q = head_rows(q_ref[rows, :], g)
        go = head_rows(grad_att[rows, :], g)
        probs = probs_at[seq, g]
        grad_probs = [
            dot_nt(go, key_rows(kv, seq, reps, tokens, KV_HEADS + g)) for kv in kv_refs
        ]
        delta = functools.reduce(
            jnp.add,
            [jnp.sum(p * d, axis=-1, keepdims=True) for p, d in zip(probs, grad_probs)],
        )
        dq = jnp.zeros((GROUP * tokens, HEAD_DIM), f32)
        for p in range(pieces):
            grad_z = (probs[p] * (grad_probs[p] - delta) * SCALE).astype(bf16)
            dq = dq + dot_nn(grad_z, key_rows(kv_refs[p], seq, reps, tokens, g))
            dk = dot_tn(grad_z, q).astype(bf16)
            dv = dot_tn(probs[p].astype(bf16), go).astype(bf16)
            stride = reps * tokens
            dkv_ref = dkv_refs[p // (pieces // 2)]
            base = p % (pieces // 2) * kv_ref.shape[1] + seq * tokens
            for a in range(dk.shape[0] // tokens):
                here = slice(base + a * stride, base + a * stride + tokens)
                part = slice(a * tokens, (a + 1) * tokens)
                dkv_ref[here, g * HEAD_DIM : (g + 1) * HEAD_DIM] = dk[part]
                v_at = (KV_HEADS + g) * HEAD_DIM
                dkv_ref[here, v_at : v_at + HEAD_DIM] = dv[part]
        for j, block in enumerate(head_columns(dq, tokens)):
            head = g * GROUP + j
            dq_ref[rows, head * HEAD_DIM : (head + 1) * HEAD_DIM] = turn(
                block, cos, -sin
            ).astype(bf16)


def attend_back(marks, gy, gain, weight, mask, cos, sin, terms, kept, reps):
    ow_pieces, starts = weight
    tokens, width = gy.shape
    pieces = len(kept) - 2
    versions = len(kept[0])
    arrays = [far(array) for item in kept for array in item]
    piece = kept[2][0]
    keys = pieces * piece.shape[0]
    return call(
        functools.partial(
            attend_back_kernel, pieces, len(ow_pieces), len(terms), reps, versions
        ),
        (
            jax.ShapeDtypeStruct((tokens, width), f32),
            jax.ShapeDtypeStruct((tokens, width), bf16),
            jax.ShapeDtypeStruct((tokens, QCOLS), bf16),
            jax.ShapeDtypeStruct((1, width), f32),
            *(jax.ShapeDtypeStruct((pieces // 2 * piece.shape[0], piece.shape[1]), bf16),) * 2,
        ),
        (marks, starts, gy, gain, mask, cos, sin, *(far(w) for w in ow_pieces), *terms, *arrays),
        2 * tokens * QCOLS * width + 30 * tokens * QCOLS * keys // reps,
        8 * keys * KCOLS + 20 * tokens * width,
        "attend_back",
        limit=20 + 40 * keys // (reps * 4096),
        in_specs=[SMEM] * 2
        + [VMEM] * 5
        + [ANY] * len(ow_pieces)
        + [VMEM] * len(terms)
        + [ANY] * len(arrays),
        out_specs=(VMEM,) * 6,
        scratch_shapes=[
            pltpu.VMEM((tokens, width), f32),
            pltpu.VMEM((tokens, QCOLS), bf16),
            pltpu.VMEM((pieces, *piece.shape), bf16),
            pltpu.SemaphoreType.DMA((2 + pieces,)),
            pltpu.VMEM((QCOLS, width), bf16),
            pltpu.SemaphoreType.DMA((1, len(ow_pieces))),
        ],
    )


def project_back_kernel(terms, reps, versions, q_count, kv_count, tile, *refs):
    (fixed, q_refs, kv_refs, t_refs, x_refs, outs, scratch), _ = taken(
        refs, (9, q_count, kv_count, terms, versions, 4, 4)
    )
    marks_ref, q_starts, kv_starts, dq_ref, gh_ref, gain_ref, mg_ref, cos_ref, sin_ref = fixed
    gin_ref, gp_ref, n_ref, small_ref = outs
    wq_ref, wkv_ref, q_sem, kv_sem = scratch
    tiles = [
        (wq_ref, k, copies)
        for k, copies in enumerate(weight_copies(q_starts, q_refs, wq_ref, q_sem, tile))
    ]
    tiles += [
        (wkv_ref, k, copies)
        for k, copies in enumerate(weight_copies(kv_starts, kv_refs, wkv_ref, kv_sem, tile))
    ]
    dkv = sum_refs(t_refs)
    cos = repeat_rows(cos_ref[...], reps)
    sin = repeat_rows(sin_ref[...], reps)
    parts = [
        turn(dkv[:, j * HEAD_DIM : (j + 1) * HEAD_DIM], cos, -sin) for j in range(KV_HEADS)
    ]
    parts.append(dkv[:, KCOLS:])
    gp_ref[:, :QCOLS] = dq_ref[...]
    gp_ref[:, QCOLS:] = jnp.concatenate(parts, axis=1).astype(bf16)
    grad_projected = gp_ref[...]
    width = gh_ref.shape[1]
    columns = gp_ref.shape[1]
    small_ref[:, width : width + columns] = jnp.sum(
        grad_projected.astype(f32), axis=0, keepdims=True
    )
    small_ref[:, width + columns :] = mg_ref[...]
    x = choose(marks_ref, x_refs).astype(f32)
    gain = gain_ref[...].astype(f32)
    n_ref[...] = (x * inverse_rms(x) * gain).astype(bf16)
    grad_normed = jnp.zeros(x.shape, f32)
    for at, (w_ref, k, copies) in enumerate(tiles):
        wait_all(copies)
        grad_normed = grad_normed + dot_nt(
            grad_projected[:, at * tile : (at + 1) * tile], w_ref[:, k * tile : (k + 1) * tile]
        )
    grad_source, grad_gain = norm_backward(grad_normed, x, gain)
    small_ref[:, :width] = grad_gain
    gin_ref[...] = (gh_ref[...] + grad_source).astype(bf16)


def project_back(marks, dq, xs, gh, gain, grad_mlp_gain, q_weight, kv_weight, cos, sin, terms, reps):
    q_pieces, q_starts = q_weight
    kv_pieces, kv_starts = kv_weight
    tokens, width = gh.shape
    columns = QCOLS + 2 * KCOLS
    tile = 2 * KCOLS
    weights = [far(w) for w in (*q_pieces, *kv_pieces)]
    return call(
        functools.partial(
            project_back_kernel, len(terms), reps, len(xs), len(q_pieces), len(kv_pieces), tile
        ),
        (
            jax.ShapeDtypeStruct((tokens, width), bf16),
            jax.ShapeDtypeStruct((tokens, columns), bf16),
            jax.ShapeDtypeStruct((tokens, width), bf16),
            jax.ShapeDtypeStruct((1, columns + 2 * width), f32),
        ),
        (marks, q_starts, kv_starts, dq, gh, gain, grad_mlp_gain, cos, sin, *weights, *terms, *xs),
        2 * tokens * width * columns,
        2 * width * columns,
        "project_back",
        limit=20,
        in_specs=[SMEM] * 3 + [VMEM] * 6 + [ANY] * len(weights) + [VMEM] * (len(terms) + len(xs)),
        out_specs=(VMEM,) * 4,
        scratch_shapes=[
            pltpu.VMEM((width, QCOLS), bf16),
            pltpu.VMEM((width, 2 * KCOLS), bf16),
            pltpu.SemaphoreType.DMA((QCOLS // tile, len(q_pieces))),
            pltpu.SemaphoreType.DMA((2 * KCOLS // tile, len(kv_pieces))),
        ],
    )


def add_kernel(parts, first, rows, *refs):
    outs = refs[len(refs) - parts :]
    total = refs[0][first : first + rows, :].astype(f32)
    for ref in refs[1 : len(refs) - parts]:
        total = total + ref[first : first + rows, :].astype(f32)
    total = total.astype(bf16)
    rows = rows // parts
    for k, out in enumerate(outs):
        out[...] = total[k * rows : (k + 1) * rows]


def add_up(terms, first, rows, parts=1, after=()):
    width = terms[0].shape[1]
    out = jax.ShapeDtypeStruct((rows // parts, width), bf16)
    return call(
        functools.partial(add_kernel, parts, first, rows),
        (out,) * parts,
        terms,
        0,
        2 * (len(terms) + 1) * rows * width,
        "add_up",
        limit=8,
        in_specs=[VMEM] * len(terms),
        after=after,
        out_specs=(VMEM,) * parts,
    )


def join_kernel(*refs):
    fill(refs[-1], refs[:-1])


def join(blocks):
    rows, width = blocks[0].shape
    return call(
        join_kernel,
        jax.ShapeDtypeStruct((rows * len(blocks), width), bf16),
        blocks,
        0,
        4 * len(blocks) * rows * width,
        "join",
        limit=4,
        in_specs=[VMEM] * len(blocks),
        out_specs=VMEM,
    )


def select_kernel(marks_ref, early_ref, late_ref, out_ref):
    out_ref[...] = choose(marks_ref, (early_ref, late_ref))


def select(marks, early, late):
    return call(
        select_kernel,
        jax.ShapeDtypeStruct(early.shape, early.dtype),
        (marks, early, late),
        0,
        6 * early.size,
        "select",
        limit=4,
        in_specs=[SMEM, VMEM, VMEM],
        out_specs=VMEM,
    )


def rows_kernel(at_ref, source, out, sem):
    rows = out.shape[0]
    at = pl.multiple_of(at_ref[0] * rows, ROWS)
    copy = pltpu.make_async_copy(source.at[pl.ds(at, rows)], out, sem)
    copy.start()
    copy.wait()


def rows_of(array, block, rows, after):
    out = jax.ShapeDtypeStruct((rows, array.shape[1]), array.dtype)
    return call(
        rows_kernel,
        out,
        (block.astype(jnp.int32).reshape(1), far(array)),
        0,
        4 * out.size,
        "rows_of",
        limit=4,
        in_specs=[SMEM, ANY],
        after=after,
        ordered=False,
        out_specs=VMEM,
        scratch_shapes=[pltpu.SemaphoreType.DMA(())],
    )


def collect_kernel(versions, *refs):
    (marks, outs, scratch) = refs[0], refs[-2], refs[-1]
    sources = refs[1:-2]
    count = len(sources) // versions
    rows = sources[0].shape[0]
    wait_all(
        bring(
            marks,
            [sources[k * versions : (k + 1) * versions] for k in range(count)],
            [outs.at[pl.ds(k * rows, rows)] for k in range(count)],
            scratch,
        )
    )


def collect(marks, early, late, after=()):
    count = len(early)
    rows, width = early[0].shape
    arrays = [a for pair in zip(early, late) for a in pair]
    return call(
        functools.partial(collect_kernel, 2),
        jax.ShapeDtypeStruct((count * rows, width), early[0].dtype),
        (marks, *arrays),
        0,
        4 * count * rows * width,
        "collect",
        limit=4,
        ordered=False,
        after=after,
        in_specs=[SMEM] + [ANY] * len(arrays),
        out_specs=ANY,
        scratch_shapes=[pltpu.SemaphoreType.DMA((count,))],
    )


def attention_grads_kernel(steps, versions, parts, *refs):
    (flags, small_refs, sources, outs, scratch), _ = taken(
        refs, (1, steps, 3 * steps + sum(versions), parts + 1, 5)
    )
    at_ref = flags[0]
    *outs, small_ref = outs
    n_ref, p_ref, a_ref, h_ref, sem = scratch
    size = n_ref.shape[0] // steps
    copies = []
    groups = []
    targets = []
    for k, target in enumerate((n_ref, p_ref, h_ref)):
        for t in range(steps):
            groups.append((sources[k * steps + t],))
            targets.append(target.at[pl.ds(t * size, size)])
    at = 3 * steps
    for t in range(steps):
        groups.append(sources[at : at + versions[t]])
        targets.append(a_ref.at[pl.ds(t * size, size)])
        at += versions[t]
    copies = bring(at_ref, groups, targets, sem)
    small_ref[...] = sum_refs(small_refs)
    wait_all(copies)
    columns = p_ref.shape[1]
    rows = outs[0].shape[0]
    for r, out in enumerate(outs):
        here = pl.ds(pl.multiple_of(at_ref[1 + r] * rows, HEAD_DIM), rows)
        out[:, :columns] = dot_tn(n_ref[:, here], p_ref[...]).astype(bf16)
        out[:, columns:] = dot_tn(a_ref[:, here], h_ref[...]).astype(bf16)


def attention_grads(marks, smalls, normed, projected, grad_hidden, attended, parts):
    steps = len(normed)
    tokens, width = normed[0].shape
    columns = projected[0].shape[1]
    rows = width // parts
    versions = [len(a) for a in attended]
    arrays = [*normed, *projected, *grad_hidden, *(a for item in attended for a in item)]
    total = steps * tokens
    return call(
        functools.partial(attention_grads_kernel, steps, versions, parts),
        (
            *(jax.ShapeDtypeStruct((rows, columns + width), bf16),) * parts,
            jax.ShapeDtypeStruct(smalls[0].shape, f32),
        ),
        (marks, *smalls, *arrays),
        2 * total * width * (columns + width),
        2 * total * (2 * width + columns) + 2 * width * (width + columns),
        "attention_grads",
        limit=40,
        in_specs=[SMEM] + [VMEM] * steps + [ANY] * len(arrays),
        out_specs=(VMEM,) * (parts + 1),
        scratch_shapes=[
            pltpu.VMEM((total, width), bf16),
            pltpu.VMEM((total, columns), bf16),
            pltpu.VMEM((total, width), bf16),
            pltpu.VMEM((total, width), bf16),
            pltpu.SemaphoreType.DMA((4 * steps,)),
        ],
    )


def assemble_kernel(pieces, *refs):
    at_ref = refs[0]
    piece_refs = refs[1 : 1 + pieces]
    left_ref, right_ref = refs[-2:]
    columns = left_ref.shape[1]
    rows = piece_refs[0].shape[0]
    for a, piece in enumerate(piece_refs):
        here = pl.ds(pl.multiple_of(at_ref[a] * rows, 8), rows)
        left_ref[here, :] = piece[:, :columns].astype(f32)
        right_ref[here, :] = piece[:, columns:].astype(f32)


def assemble(places, pieces, columns, after):
    rows, total = pieces[0].shape
    count = len(pieces)
    return call(
        functools.partial(assemble_kernel, count),
        (
            jax.ShapeDtypeStruct((rows * count, columns), f32),
            jax.ShapeDtypeStruct((rows * count, total - columns), f32),
        ),
        (places, *pieces),
        0,
        6 * rows * count * total,
        "assemble",
        limit=24,
        in_specs=[SMEM] + [VMEM] * count,
        after=after,
        ordered=False,
        out_specs=(VMEM, VMEM),
    )


def unit_tile(units, most):
    return max(t for t in range(16, most + 1, 16) if units % t == 0)


def weight_grad_kernel(aliased, adds, *refs):
    n_ref, g_ref, gate_ref, up_ref, down_ref = refs[:5]
    olds = refs[5 : 5 + aliased]
    news = refs[-4:-1]
    refs[-1][...] = jnp.zeros_like(refs[-1])

    @pl.when(pl.program_id(1) == 0)
    def _():
        for k, new in enumerate(news):
            new[...] = olds[k][...] if adds else jnp.zeros_like(new)

    rows = n_ref[...]
    grads = g_ref[...]
    gate_pre = dot_nt(gate_ref[...], rows)
    up_pre = dot_nt(up_ref[...], rows)
    grad_act = dot_nt(down_ref[...], grads)
    silu, grad_gate, grad_up = swiglu_backward(gate_pre, up_pre, grad_act)
    activated = (silu * up_pre).astype(bf16)
    news[0][...] += dot_nn(grad_gate, rows)
    news[1][...] += dot_nn(grad_up, rows)
    news[2][...] += dot_nn(activated, grads)


def weight_grads(n_all, g_all, gate, up, down, outs, adds, first, count, after):
    units, width = gate.shape
    tokens = n_all.shape[0]
    tile = unit_tile(units, 320)
    chunk = math.gcd(tokens, 1024)
    shape = jax.ShapeDtypeStruct((units, width), f32)
    part = pl.BlockSpec((tile, width), lambda i, j: (i + first, 0))
    rows = pl.BlockSpec((chunk, width), lambda i, j: (j, 0))
    *outs, zeros = call(
        functools.partial(weight_grad_kernel, len(outs), adds),
        (*(shape,) * 3, jax.ShapeDtypeStruct((8, 128), f32)),
        (n_all, g_all, gate, up, down, *outs),
        12 * tokens * width * tile * count,
        18 * width * tile * count,
        "weight_grads",
        limit=60,
        ordered=False,
        grid=(count, tokens // chunk),
        in_specs=[rows] * 2
        + [part] * 3
        + [part if adds else ANY] * len(outs),
        after=after,
        out_specs=((*(part,) * 3, pl.BlockSpec((8, 128), lambda i, j: (0, 0)))),
        input_output_aliases={len(after) + 5 + k: k for k in range(len(outs))},
    )
    return outs, zeros


def body(
    inputs,
    cotangent,
    attn_gain,
    qkv_weight,
    qkv_bias,
    out_weight,
    mlp_gain,
    gate_weight,
    up_weight,
    down_weight,
):
    first = lax.axis_index("section") == 0
    micro, rows_here, _, width = inputs.shape
    fsdp = lax.axis_size("fsdp")
    ctx = lax.axis_size("ctx")
    fsdp_at = lax.axis_index("fsdp")
    ctx_at = lax.axis_index("ctx")
    tokens = 2 * rows_here
    reps = MICROS
    chunks = micro // reps
    steps = chunks + LAG
    span_rows = rows_here * fsdp
    half_rows = span_rows * ctx

    def places_of(c, f, token):
        index = (c * fsdp + f) * rows_here + token // 2
        second = 2 * half_rows - span_rows * (index // span_rows + 1) + index % span_rows
        return jnp.where(token % 2 == 0, index, second)

    own = places_of(ctx_at, fsdp_at, jnp.arange(tokens, dtype=jnp.int32))
    shape = (fsdp, tokens, ctx * tokens)
    number = lax.broadcasted_iota(jnp.int32, shape, 0)
    other = jnp.zeros(shape, jnp.int32)
    for k, r in enumerate(relative_order(fsdp)):
        other = jnp.where(number == k, fsdp_at ^ r, other)
    column = lax.broadcasted_iota(jnp.int32, shape, 2)
    key_places = places_of(ctx_at ^ (column // tokens), other, column % tokens)
    query_places = places_of(ctx_at, fsdp_at, lax.broadcasted_iota(jnp.int32, shape, 1))
    mask = jnp.where(key_places <= query_places, 0.0, NEGATIVE).astype(f32)
    half = HEAD_DIM // 2
    frequency = ROPE_BASE ** (-(jnp.arange(half, dtype=f32) * 2.0) / HEAD_DIM)
    angles = own.astype(f32)[:, None] * frequency
    cos = jnp.concatenate([jnp.cos(angles)] * 2, axis=1)
    sin = jnp.concatenate([-jnp.sin(angles), jnp.sin(angles)], axis=1)

    packed = jnp.concatenate([attn_gain, qkv_bias, mlp_gain], axis=1)
    packed_pieces = gather_pieces(packed, "fsdp")
    owners = jnp.arange(fsdp, dtype=jnp.int32)[:, None]
    packed = functools.reduce(
        jnp.add,
        [
            jnp.where(owners == fsdp_at ^ r, piece, jnp.zeros_like(piece))
            for r, piece in zip(relative_order(fsdp), packed_pieces)
        ],
    )
    gain_part, bias_part = attn_gain.shape[1], qkv_bias.shape[1]
    attn_full = packed[:, :gain_part].reshape(1, -1)
    bias_full = packed[:, gain_part : gain_part + bias_part].reshape(1, -1)
    mlp_full = packed[:, gain_part + bias_part :].reshape(1, -1)

    def gathered(shard, after=None):
        units = shard.shape[0] // ROWS
        pieces = [(shard, fsdp_at * units)]
        for bit in bits_of(fsdp):
            if len(pieces) == 1 and after is not None:
                half = units // 2
                odd = ctx_at & 1
                mine = exchange(rows_of(shard, odd, half * ROWS, after), "fsdp", bit)
                other = exchange(mine, "ctx", 1)
                base = (fsdp_at ^ bit) * units
                pieces += [(mine, base + odd * half), (other, base + (1 - odd) * half)]
            else:
                pieces += [
                    (exchange(piece, "fsdp", bit), (at // units ^ bit) * units + at % units)
                    for piece, at in pieces
                ]
        starts = jnp.stack([at.astype(jnp.int32) for _, at in pieces])
        return [piece for piece, _ in pieces], starts

    kv_weight = gathered(qkv_weight[0, :, QCOLS:])
    q_weight = gathered(qkv_weight[0, :, :QCOLS], kv_weight[0][1:2])
    gate, up, down = gate_weight[0], up_weight[0], down_weight[0]
    flag = first.astype(jnp.int32)
    marks = jnp.stack([flag] + [(fsdp_at ^ r).astype(jnp.int32) for r in relative_order(fsdp)])

    def chunked(array):
        return array.reshape(chunks, reps * tokens, width)

    in_chunks = chunked(inputs)
    cot_chunks = chunked(cotangent)

    def pick(early, late):
        return jnp.where(first, early, late)

    def versions(u, early, late):
        if u < LAG:
            return (late[u + LAG],)
        if u < chunks:
            return (early[u - LAG], late[u + LAG])
        return (early[u - LAG],)

    gys = [jnp.where(first, jnp.zeros_like(cot), cot) for cot in cot_chunks[:LAG]]
    early_pieces = [gather_pieces(gy, "fsdp") for gy in gys]
    gys = dict(enumerate(gys))

    ORDER.clear()

    def pick(early, late):
        return jnp.where(first, early, late)

    def versions(u, early, late):
        if u < LAG:
            return (late[u + LAG],)
        if u < chunks:
            return (early[u - LAG], late[u + LAG])
        return (early[u - LAG],)


    first_keys, out_weights = [], []
    near_weights = [gate, up, down]
    outputs, moved, xs, kept, attended, n2_pieces = {}, {}, {}, {}, {}, {}
    grads_in, grads_moved, smalls, factors = {}, {}, {}, {}

    def add_one(terms, rows):
        return add_up(terms, rows, rows)[0]

    def forward(t):
        if t < LAG:
            x = (in_chunks[t],)
        elif t < chunks:
            x = (in_chunks[t], moved[t])
        else:
            x = (moved[t],)
        xs[t] = x
        kv = project(
            marks, x, attn_full, kv_weight, bias_full[:, QCOLS:], cos, sin, reps, KV_HEADS
        )
        first_keys.append(kv)
        blocks = [kv] + [exchange(kv, "ctx", a) for a in range(1, ctx)]
        yield "K"
        for name in "QJ" if LAG <= t < chunks else "JQ":
            if name == "J":
                kv_pieces = gather_pieces(join(blocks), "fsdp")
            else:
                q = project(
                    marks, x, attn_full, q_weight, bias_full[:, :QCOLS], cos, sin, reps, HEADS
                )
            yield name
        if t == 0:
            out_weights.extend(gathered(out_weight[0], first_keys))
        after = [p for pieces in early_pieces for p in pieces[1:]] if t == LAG else []
        att, hidden, n2 = attend(
            marks, q, x, mask, out_weights, mlp_full, kv_pieces, reps, after
        )
        attended[t] = att
        n2_pieces[t] = gather_pieces(n2, "fsdp")
        kept[t] = (hidden, q, *kv_pieces)
        yield "A"
        parts = mlp(n2_pieces[t], *near_weights)
        terms = yield from stages(reduction(*parts, "fsdp", add_one), "M", "R")
        outputs[t] = add_up([hidden, *terms], 0, hidden.shape[0])[0]
        if t < chunks:
            moved[t + LAG] = passed_along(outputs[t], "section", 1)
        yield "Y"

    def stages(generator, first_name, name):
        while True:
            try:
                next(generator)
            except StopIteration as end:
                return end.value
            yield first_name
            first_name = name

    def backward(u):
        if u < LAG:
            gy, g_pieces = gys[u], early_pieces[u]
        else:
            gy = select(marks, grads_moved[u], cot_chunks[u]) if u < chunks else grads_moved[u]
            gys[u] = gy
            g_pieces = gather_pieces(gy, "fsdp")
            yield "G"
        n2_now = list(zip(*versions(u, n2_pieces, n2_pieces)))
        parts = mlp_back(marks, n2_now, g_pieces, *near_weights, [])
        terms = yield from stages(reduction(*parts, "fsdp", add_one), "B", "S")
        kept_now = list(zip(*versions(u, kept, kept)))
        gh, gh_low, dq, grad_mlp_gain, *dkv = attend_back(
            marks, gy, mlp_full, out_weights, mask, cos, sin, terms, kept_now, reps
        )
        terms = yield from stages(reduction(*dkv, "fsdp", add_one), "T", "D")
        own, *others = add_up(terms, 0, ctx * reps * tokens, ctx)
        dkv_terms = [own] + [exchange(other, "ctx", a + 1) for a, other in enumerate(others)]
        yield "E"
        x_now = versions(u, {t: x[0] for t, x in xs.items()}, {t: x[-1] for t, x in xs.items()})
        g_in, g_proj, normed, small = project_back(
            marks,
            dq,
            x_now,
            gh,
            attn_full,
            grad_mlp_gain,
            q_weight,
            kv_weight,
            cos,
            sin,
            dkv_terms,
            reps,
        )
        grads_in[u] = g_in
        if u < chunks:
            grads_moved[u + LAG] = passed_along(g_in, "section", -1)
        smalls[u] = small
        factors[u] = (normed, g_proj, gh_low, versions(u, attended, attended))
        yield "P"

    running = {}
    for name in SEQUENCE:
        if name == "H":
            near_weights[:] = hold(gate, up, down)
            continue
        kind, step = name[0], int(name[1:])
        key = (kind in FORWARD, step)
        if key not in running:
            running[key] = forward(step) if key[0] else backward(step)
        while next(running[key]) != kind:
            pass
    grads_in, gys, smalls, factors = (
        [found[t] for t in range(steps)] for found in (grads_in, gys, smalls, factors)
    )

    batches = [b for b in (range(0, chunks // 2), range(chunks // 2, chunks)) if len(b)]

    def all_tokens(early, late, batch):
        own_rows = collect(marks, [early[m] for m in batch], [late[m] for m in batch])
        return lax.all_gather(own_rows, ("ctx", "fsdp"), axis=0, tiled=True)

    n2_own = [n2_pieces[t][0] for t in range(steps)]
    n2_all = [all_tokens(n2_own, n2_own[LAG:], batch) for batch in batches]
    g_all = [all_tokens(gys[LAG:], gys, batch) for batch in batches]
    tiles = gate.shape[0] // unit_tile(gate.shape[0], 320)
    cuts = [0, tiles // 7, 6 * tiles // 7, tiles], [0, 3 * tiles // 7, tiles]
    plan = [
        (b, i, j - i)
        for b in range(len(batches))
        for i, j in zip(cuts[b], cuts[b][1:])
        if j > i
    ]
    mlp_grads = []

    def some_weight_grads(after):
        nonlocal mlp_grads
        if not plan:
            return None
        b, start, count = plan.pop(0)
        mlp_grads, zeros = weight_grads(
            n2_all[b], g_all[b], gate, up, down, mlp_grads, b > 0, start, count, after
        )
        return zeros

    lead = QCOLS + KCOLS
    columns = QCOLS + 2 * KCOLS
    normed, projected, grad_hidden, att_now = zip(*factors)
    rows = width // fsdp
    if rows % HEAD_DIM == 0:
        *summed, small = attention_grads(
            marks, smalls, normed, projected, grad_hidden, att_now, fsdp
        )
    else:
        start = jnp.stack([flag, jnp.int32(0)])
        large, small = attention_grads(
            start, smalls, normed, projected, grad_hidden, att_now, 1
        )
        summed = [
            lax.dynamic_slice_in_dim(large, (fsdp_at ^ r) * rows, rows)
            for r in relative_order(fsdp)
        ]
    small = small.reshape(-1, HEAD_DIM)
    for bit in reversed(bits_of(fsdp)):
        count = len(summed) // 2
        moves = [exchange(p, "fsdp", bit) for p in summed[count:]]
        zeros = some_weight_grads(summed[:1])
        zero = 0.0 if zeros is None else zeros[0, 0]
        small = small + zero
        summed = [
            (p.astype(f32) + m.astype(f32) + zero).astype(bf16) for p, m in zip(summed, moves)
        ]
        small = small + exchange(small, "fsdp", bit)
    rows = width // fsdp // ctx
    terms = [
        lax.dynamic_slice_in_dim(summed[0], (ctx_at ^ a) * rows, rows) for a in range(ctx)
    ]
    moves = [exchange(terms[a], "ctx", a) for a in range(1, ctx)]
    small = small + exchange(small, "ctx", bits_of(ctx)[0])
    zeros = some_weight_grads(terms[:1])
    zeros = some_weight_grads([]) if plan else zeros
    block = functools.reduce(jnp.add, [t.astype(f32) for t in (terms[0], *moves)])
    small = small + (0.0 if zeros is None else zeros[0, 0])
    block = (block + (0.0 if zeros is None else zeros[0, 0])).astype(bf16)
    pieces = [block] + [exchange(block, "ctx", a) for a in range(1, ctx)]
    for bit in bits_of(ctx)[1:]:
        small = small + exchange(small, "ctx", bit)
    zeros = some_weight_grads([block])
    places = jnp.stack([(ctx_at ^ a).astype(jnp.int32) for a in range(ctx)])
    ends = [] if zeros is None else [zeros]
    grad_qkv, grad_out = assemble(places, pieces, columns, [] if zeros is None else [zeros])
    while plan:
        some_weight_grads([])
    grad_gate, grad_up, grad_down = mlp_grads

    small = small.reshape(-1)

    def cut(start, length):
        part = length // fsdp
        return lax.dynamic_slice(small, (start + fsdp_at * part,), (part,))

    grad_attn_gain = cut(0, width)
    grad_bias_lead = cut(width, lead)
    grad_bias_value = cut(width + lead, columns - lead)
    grad_mlp_gain = cut(width + columns, width)

    for generator in running.values():
        for _ in generator:
            pass
    outputs = [outputs[t] for t in range(steps)]
    layer_outputs = collect(marks, outputs[:chunks], outputs[LAG:], ends).reshape(inputs.shape)
    input_grads = collect(marks, grads_in[LAG:], grads_in[:chunks], ends).reshape(inputs.shape)
    return (
        layer_outputs[None],
        input_grads[None],
        grad_attn_gain[None],
        grad_qkv[None],
        grad_bias_lead[None],
        grad_bias_value[None],
        grad_out[None],
        grad_mlp_gain[None],
        grad_gate[None],
        grad_up[None],
        grad_down[None],
    )


def solution(mesh):
    rows = P(None, ("ctx", "fsdp"), None, None)
    vector = P("section", "fsdp")
    matrix = P("section", "fsdp", None)
    stacked = P("section", None, ("ctx", "fsdp"), None, None)
    in_specs = (rows, rows, vector, matrix, vector, matrix, vector, matrix, matrix, matrix)
    out_specs = (
        stacked,
        stacked,
        vector,
        matrix,
        vector,
        vector,
        matrix,
        vector,
        matrix,
        matrix,
        matrix,
    )
    return jax.shard_map(body, mesh=mesh, in_specs=in_specs, out_specs=out_specs, check_vma=False)
```
